256 devices in a mesh: seq: 128 (over z, y, x), head: 2 (over core).
Axes of the slice: x: 4, y: 4, z: 8, core: 2. Of those that a mesh axis runs over, the one named last changes fastest.
Arguments:
- query_vectors: bfloat16 [16384, 2048], P('seq', 'head'), may hold values from -12 to 12
- key_vectors: bfloat16 [16384, 2048], P('seq', 'head'), may hold values from -12 to 12
- value_vectors: bfloat16 [16384, 2048], P('seq', 'head'), may hold values from -6 to 6
- cotangent: bfloat16 [16384, 2048], P('seq', 'head'), may hold values from -24 to 24
- rand_peer: int32 [2, 256, 8, 3], P('head', 'seq'), may hold values from 0 to 127, all different within a row; in each aligned block of 16 rows (0 to 15, 16 to 31, ..., all dimensions but the last counted through in order) at most 2 rows name the same one
- rand_local: int32 [2, 256, 8, 3], P('head', 'seq'), may hold values from 0 to 1
- global_ids: int32 [2], replicated, may hold values from 0 to 255, as said below
Outputs:
- attended: bfloat16 [16384, 2048], P(('seq', 'head'))
- grad_query: bfloat16 [16384, 2048], P(('seq', 'head'))
- grad_key: bfloat16 [16384, 2048], P(('seq', 'head'))
- grad_value: bfloat16 [16384, 2048], P(('seq', 'head'))
The draws below stay inside these ranges and needn't reach their ends.
Inputs may be any that keep to these rules, and one draw needn't show every extreme that they name: `rand_peer`: per head group, query block and head, three different numbers. Among the 48 entries of one index of seq and head, no number appears more than 2 times; in some such rows one appears exactly 2 times. `global_ids`: two different blocks; one of them, in either place, is the last block 255.
All inputs are finite; a program needn't handle non-finite values.
Results may differ from the reference program's by a relative error of at most 0.0065.
Values may be sent and summed in bfloat16 or wider, within the bound.
A program may use at most 128 MiB of HBM per device.

```python
import math
import jax
import jax.numpy as jnp
import numpy as np
from jax import lax

HEADS = 16
HEAD_DIM = 128
BLOCK = 64
D = 2048
HEADS_DEV = 8
BLK_DEV = 2
NB = 256
LENGTH = 16384
MOST = 2
N_SEQ = 128
N_HEAD = 2


def draw_query_vectors(key, part):
    key = jax.random.fold_in(key, 11)
    return (1.5 * jax.random.truncated_normal(key, -8.0, 8.0, (LENGTH, D), jnp.float32)).astype(jnp.bfloat16)


def draw_key_vectors(key, part):
    key = jax.random.fold_in(key, 12)
    return (1.5 * jax.random.truncated_normal(key, -8.0, 8.0, (LENGTH, D), jnp.float32)).astype(jnp.bfloat16)


def draw_global_ids(key, part):
    key = jax.random.fold_in(key, 13)
    other_key, coin_key = jax.random.split(key)
    other = jax.random.randint(other_key, (), 0, NB - 1, dtype=jnp.int32)
    last = jnp.array(NB - 1, jnp.int32)
    coin = jax.random.randint(coin_key, (), 0, 2, dtype=jnp.int32)
    first = jnp.where(coin == 0, other, last)
    second = jnp.where(coin == 0, last, other)
    return jnp.stack([first, second]).astype(jnp.int32)


def touch_ends(drawn, rng, least, largest):
    longest = drawn.shape.index(max(drawn.shape))
    spots = []
    for shift in (0, 1):
        where = [jax.random.randint(jax.random.fold_in(rng, axis), (), 0, length) for axis, length in enumerate(drawn.shape)]
        where[longest] = (where[longest] + shift) % drawn.shape[longest]
        spots.append(tuple(where))
    return drawn.at[spots[0]].set(least).at[spots[1]].set(largest)


def block_levels(stream_key, extent, cuts, smallest, top_value):
    def one(dim, parts):
        draws = jax.random.uniform(jax.random.fold_in(jax.random.fold_in(stream_key, 6), dim), (parts,), jnp.float32, smallest / len(cuts), top_value / len(cuts))
        return jnp.repeat(jnp.exp(draws), extent[dim] // parts).reshape((-1,) + (1,) * (len(extent) - dim - 1))

    level = one(*cuts[0])
    for cut in cuts[1:]:
        level = level * one(*cut)
    return level


def deal_out(key, own, number, rows, number_of, top, most, lean):
    sequence = jax.random.permutation(key, number_of)
    packed, usual = load_shares(number_of, rows * top, most, lean, True), load_shares(number_of, rows * top, most, lean, False)
    places = jnp.arange(number_of)

    def named(sizes, offset_by):
        used = int((sizes > 0).sum())
        fixed = max(1, used // 4)
        shifted = fixed + (places - fixed + offset_by * (used - fixed)) % max(1, number_of - fixed)
        return jnp.zeros((number_of,), jnp.int32).at[sequence[jnp.where(places < fixed, places, shifted)]].set(jnp.asarray(sizes, jnp.int32))

    sizes = jnp.where(number % 4 == 0, named(packed, number // 4), named(usual, number - number // 4 - 1))
    mixed = jax.random.permutation(jax.random.fold_in(own, 3), number_of)
    donor, receiver = mixed[0:number_of // 2 * 2:2], mixed[1:number_of // 2 * 2:2]
    margin = jnp.minimum(sizes[donor] - 1, most - sizes[receiver]) // 2
    margin = jnp.where((donor == sequence[0]) | (receiver == sequence[0]) | (sizes[receiver] == 0), 0, jnp.maximum(margin, 0))
    shifted = jax.random.randint(jax.random.fold_in(own, 4), (number_of // 2,), 0, 1 << 20) % (margin + 1)
    sizes = sizes.at[donor].add(-shifted).at[receiver].add(shifted)
    items = jnp.searchsorted(jnp.cumsum(sizes), jnp.arange(rows * top), side="right").astype(jnp.int32)
    table = items.reshape(top, rows).T
    table = table[jax.random.permutation(jax.random.fold_in(own, 1), rows)]
    offset_by = jax.random.randint(jax.random.fold_in(own, 2), (rows, 1), 0, top)
    return jnp.take_along_axis(table, (jnp.arange(top)[None, :] + offset_by) % top, axis=1)


def load_shares(amount, total, most, skew, full):
    portions = [(1 << 20) // math.isqrt(grade ** skew) + 1 for grade in range(1, amount + 1)]
    largest = most if full else min(most, max(-(-total // amount), total * portions[0] // sum(portions)))
    least = 1 if total - largest >= amount - 1 else 0
    counts, surplus = [largest] + [least] * (amount - 1), total - largest - least * (amount - 1)
    while surplus > 0:
        candidates = [i for i in range(1, amount) if counts[i] < largest] or [i for i in range(1, amount) if counts[i] < most]
        mass, left = sum([portions[i] for i in candidates]), surplus
        for i in candidates:
            extra = min(most - counts[i], max(1, left * portions[i] // mass), surplus)
            counts[i] = counts[i] + extra
            surplus = surplus - extra
    return np.array(counts)


def scatter_about(rng, shape, width, reach, cuts=(), kind=jnp.bfloat16):
    values = width * jax.random.normal(rng, shape, jnp.float32)
    if cuts:
        values = values * block_levels(rng, shape, cuts, -0.22, 0.18)
    return jnp.clip(values, -reach, reach).astype(kind)


def setup_inputs(seed: int = 0) -> dict:
    streams_of = jax.random.split(jax.random.key(seed), 8)
    query_vectors = draw_query_vectors(jax.random.fold_in(streams_of[7], 71), 0)
    key_vectors = draw_key_vectors(jax.random.fold_in(streams_of[7], 71), 0)
    value_vectors = scatter_about(streams_of[2], (LENGTH, D), 1.0, 6.0, ((0, 128), (1, 2)))
    cotangent = scatter_about(streams_of[3], (LENGTH, D), 4.0, 24.0, ((0, 128), (1, 2)))
    rand_peer_keys = jax.random.split(jax.random.fold_in(streams_of[4], 1), N_HEAD * NB * HEADS_DEV // (BLK_DEV * HEADS_DEV))
    rand_peer_turns = jax.random.permutation(jax.random.fold_in(streams_of[4], 3), N_HEAD * NB * HEADS_DEV // (BLK_DEV * HEADS_DEV))
    rand_peer = jax.vmap(lambda own, number: deal_out(jax.random.fold_in(streams_of[4], 2), own, number, BLK_DEV * HEADS_DEV, N_SEQ, 3, MOST, 2))(rand_peer_keys, rand_peer_turns).reshape((N_HEAD, NB, HEADS_DEV, 3))
    rand_local = touch_ends(jax.random.randint(streams_of[5], (N_HEAD, NB, HEADS_DEV, 3), 0, BLK_DEV), jax.random.fold_in(streams_of[5], 1), 0, BLK_DEV - 1).astype(jnp.int32)
    global_ids = draw_global_ids(jax.random.fold_in(streams_of[7], 71), 0)
    return {"query_vectors": query_vectors, "key_vectors": key_vectors, "value_vectors": value_vectors, "cotangent": cotangent, "rand_peer": rand_peer, "rand_local": rand_local, "global_ids": global_ids}


def head_columns(source_array, head_number):
    picked = lax.dynamic_slice_in_dim(source_array, head_number * HEAD_DIM, HEAD_DIM, 1)
    return picked.astype(jnp.float32).reshape(NB, BLOCK, HEAD_DIM)


def round_random(terms):
    split = terms.reshape(NB, 8, BLOCK, HEAD_DIM)
    lowered = lax.optimization_barrier(split.astype(jnp.bfloat16)).astype(jnp.float32)
    places = jnp.arange(8, dtype=jnp.int32)
    is_random = jnp.logical_and(places >= 3, places < 6)
    return jnp.where(is_random[None, :, None, None], lowered, split).reshape(NB * 8, BLOCK, HEAD_DIM)


def reference(query_vectors, key_vectors, value_vectors, cotangent, rand_peer, rand_local, global_ids):
    score_scale = HEAD_DIM ** -0.5
    block_ids = jnp.arange(NB, dtype=jnp.int32)
    left_ids = jnp.maximum(block_ids - 1, 0)
    right_ids = jnp.minimum(block_ids + 1, NB - 1)
    always = jnp.ones((NB,), bool)
    valid_blocks = jnp.stack([block_ids > 0, always, block_ids < NB - 1, always, always, always, always, always], axis=1)
    key_mask = jnp.repeat(valid_blocks, BLOCK, axis=1)

    def single_head(head_number):
        group = head_number // HEADS_DEV
        inner = head_number % HEADS_DEV
        random_ids = rand_peer[group, :, inner, :] * BLK_DEV + rand_local[group, :, inner, :]
        global_cols = jnp.broadcast_to(global_ids[None, :], (NB, 2))
        key_list = jnp.concatenate([left_ids[:, None], block_ids[:, None], right_ids[:, None], random_ids, global_cols], axis=1).astype(jnp.int32)
        block_query_rows = head_columns(query_vectors, head_number)
        key_block = head_columns(key_vectors, head_number)
        value_block = head_columns(value_vectors, head_number)
        block_gradient = head_columns(cotangent, head_number)
        keys_listed = key_block[key_list].reshape(NB, 8 * BLOCK, HEAD_DIM)
        values_listed = value_block[key_list].reshape(NB, 8 * BLOCK, HEAD_DIM)
        logits = jnp.einsum("nqd,nkd->nqk", block_query_rows, keys_listed, precision=lax.Precision.HIGHEST) * score_scale
        logits = jnp.where(key_mask[:, None, :], logits, -jnp.inf)
        row_top = jnp.max(logits, axis=-1, keepdims=True)
        log_total = row_top + jnp.log(jnp.sum(jnp.exp(logits - row_top), axis=-1, keepdims=True))
        weights = jnp.exp(logits - log_total)
        weights_reduced_precision = lax.optimization_barrier(weights.astype(jnp.bfloat16)).astype(jnp.float32)
        attended = jnp.einsum("nqk,nkd->nqd", weights_reduced_precision, values_listed, precision=lax.Precision.HIGHEST)
        grad_weights = jnp.einsum("nqd,nkd->nqk", block_gradient, values_listed, precision=lax.Precision.HIGHEST)
        centre = jnp.sum(weights * grad_weights, axis=-1, keepdims=True)
        logit_gradient = lax.optimization_barrier((weights * (grad_weights - centre) * score_scale).astype(jnp.bfloat16)).astype(jnp.float32)
        grad_query = jnp.einsum("nqk,nkd->nqd", logit_gradient, keys_listed, precision=lax.Precision.HIGHEST)
        key_terms = jnp.einsum("nqk,nqd->nkd", logit_gradient, block_query_rows, precision=lax.Precision.HIGHEST)
        value_terms = jnp.einsum("nqk,nqd->nkd", weights_reduced_precision, block_gradient, precision=lax.Precision.HIGHEST)
        flat_ids = key_list.reshape(NB * 8)
        grad_key = jnp.zeros((NB, BLOCK, HEAD_DIM), jnp.float32).at[flat_ids].add(round_random(key_terms))
        grad_value = jnp.zeros((NB, BLOCK, HEAD_DIM), jnp.float32).at[flat_ids].add(round_random(value_terms))
        return (attended.astype(jnp.bfloat16), grad_query.astype(jnp.bfloat16), grad_key.astype(jnp.bfloat16), grad_value.astype(jnp.bfloat16))

    results = lax.map(single_head, jnp.arange(HEADS, dtype=jnp.int32))

    def assemble(stacked):
        return stacked.transpose(1, 2, 0, 3).reshape(LENGTH, D)

    return (assemble(results[0]), assemble(results[1]), assemble(results[2]), assemble(results[3]))
```

```python
import functools

import jax
import jax.numpy as jnp
from jax import lax
from jax.experimental import pallas as pl
from jax.experimental.pallas import tpu as pltpu
from jax.sharding import PartitionSpec as P

MESH = pl.DeviceIdType.MESH
HEAD_DIM = 128
BLOCK = 64
HEADS_HERE = 8
BLOCKS_HERE = 2
WIDTH = HEADS_HERE * HEAD_DIM
PLANE = 16
DEPTH = 8
ITEMS = BLOCKS_HERE * HEADS_HERE
PICKS = 3 * ITEMS
ROWS = 32
CHUNKS = 4
VMEM_BYTES = 56 * 1024 * 1024
F32 = jnp.float32
BF16 = jnp.bfloat16


def position():
    seq = lax.axis_index("seq")
    return seq, lax.div(seq, PLANE), lax.rem(seq, PLANE), lax.axis_index("head")


def signal(seq, head):
    pl.semaphore_signal(
        pltpu.get_barrier_semaphore(), inc=1, device_id=(seq, head), device_id_type=MESH
    )


def remote(src, dst, send, recv, seq, head):
    return pltpu.make_async_remote_copy(
        src_ref=src,
        dst_ref=dst,
        send_sem=send,
        recv_sem=recv,
        device_id=(seq, head),
        device_id_type=MESH,
    )


def swap_tables_kernel(table, got, most, send1, recv1, send2, recv2):
    seq, z, p, head = position()
    place = z * 2 + head

    def plane_copy(i):
        peer = lax.rem(p + i, PLANE)
        return remote(
            table.at[peer], got.at[p], send1.at[i], recv1.at[i], z * PLANE + peer, head
        )

    def column_copy(i):
        other = lax.rem(place + i, 2 * DEPTH)
        return remote(
            most.at[place],
            most.at[place],
            send2.at[i],
            recv2.at[i],
            lax.div(other, 2) * PLANE + p,
            lax.rem(other, 2),
        )

    @pl.loop(1, PLANE)
    def _(i):
        signal(z * PLANE + lax.rem(p + i, PLANE), head)
        other = lax.rem(place + i, 2 * DEPTH)
        signal(lax.div(other, 2) * PLANE + p, lax.rem(other, 2))

    pl.semaphore_wait(pltpu.get_barrier_semaphore(), 2 * (PLANE - 1))

    @pl.loop(1, PLANE)
    def _(i):
        plane_copy(i).start()

    got[p] = table[p]

    @pl.loop(1, PLANE)
    def _(i):
        plane_copy(i).wait()

    most[place] = jnp.max(got[...], axis=0)

    @pl.loop(1, 2 * DEPTH)
    def _(i):
        column_copy(i).start()

    @pl.loop(1, 2 * DEPTH)
    def _(i):
        column_copy(i).wait()


def swap_tables(table):
    shape = jax.ShapeDtypeStruct((PLANE, 8, 128), jnp.int32)
    vmem = pl.BlockSpec(memory_space=pltpu.VMEM)
    return pl.pallas_call(
        swap_tables_kernel,
        out_shape=(shape, shape),
        in_specs=[vmem],
        out_specs=(vmem, vmem),
        scratch_shapes=[pltpu.SemaphoreType.DMA((PLANE,))] * 4,
        compiler_params=pltpu.CompilerParams(collective_id=0, has_side_effects=True),
        name="swap_tables",
    )(table)


def greet(z, p, seq, head, partner):
    @pl.loop(1, PLANE)
    def _(i):
        signal(z * PLANE + lax.rem(p + i, PLANE), head)

    for step in (1, DEPTH - 1):
        signal(lax.rem(z + step, DEPTH) * PLANE + p, head)
    for step in (1, PLANE * DEPTH - 1):
        signal(lax.rem(seq + step, PLANE * DEPTH), head)
    if partner:
        signal(seq, 1 - head)
    pl.semaphore_wait(pltpu.get_barrier_semaphore(), PLANE + 3 + (1 if partner else 0))


def ring_hops(q, d):
    return 4 if (d == 0) == (q % 2 == 0) else 3


def ring_slot(q, d, t):
    return sum(ring_hops(q, e) for e in range(d)) + 7 * q + t


def fetch_kernel(c, slots, glob, key, value, halo, shared, *rest):
    picked, held, out = rest[0:4], rest[4:8], rest[8:12]
    relay, zsend, zrecv, psend, precv, gsend, grecv, hsend, hrecv = rest[12:]
    seq, z, p, head = position()
    greet(z, p, seq, head, False)

    def halo_copy(side, kv):
        block = (1 - side) * BLOCK
        other = lax.rem(seq + (1 if side == 0 else PLANE * DEPTH - 1), PLANE * DEPTH)
        return remote(
            (key, value)[kv].at[pl.ds(block, BLOCK)],
            halo.at[side * 2 + kv],
            hsend.at[side * 2 + kv],
            hrecv.at[side * 2 + kv],
            other,
            head,
        )

    def ring_copy(q, d, t):
        step = 1 if d == 0 else DEPTH - 1
        owner = lax.rem(z + t * (DEPTH - step), DEPTH)
        rows = pl.ds(owner * ITEMS, ITEMS)
        slot = ring_slot(q, d, t)
        return remote(
            held[q].at[rows],
            held[q].at[rows],
            zsend.at[slot],
            zrecv.at[slot],
            lax.rem(z + step, DEPTH) * PLANE + p,
            head,
        )

    def plane_copy(q, i):
        peer = lax.rem(p + i, PLANE)
        return remote(
            out[q].at[pl.ds(peer * (c + 1), c + 1)],
            picked[q].at[pl.ds(p * (c + 1), c + 1)],
            psend.at[q * PLANE + i],
            precv.at[q * PLANE + i],
            z * PLANE + peer,
            head,
        )

    def shared_copy(q, i):
        peer = lax.rem(p + i, PLANE)
        return remote(
            relay.at[q],
            shared.at[q * PLANE + p],
            gsend.at[q * PLANE + i],
            grecv.at[q * PLANE + i],
            z * PLANE + peer,
            head,
        )

    def fill(q):
        source, half = (key, value)[q // 2], q % 2
        for b in range(BLOCKS_HERE):
            for j in range(HEADS_HERE):
                held[q][z * ITEMS + b * HEADS_HERE + j] = source[
                    b * BLOCK + half * ROWS : b * BLOCK + (half + 1) * ROWS,
                    j * HEAD_DIM : (j + 1) * HEAD_DIM,
                ]

    def ring_start(q):
        for d in range(2):
            ring_copy(q, d, 0).start()

    def ring(chunks):
        for t in range(4):
            for q in chunks:
                for d in range(2):
                    if t < ring_hops(q, d):
                        ring_copy(q, d, t).wait_recv()
                        if t + 1 < ring_hops(q, d):
                            ring_copy(q, d, t + 1).start()

    def spread(q):
        @pl.loop(1, PLANE)
        def _(i):
            peer = lax.rem(p + i, PLANE)
            for s in range(c):
                out[q][peer * (c + 1) + s] = held[q][slots[peer, s]]
            out[q][peer * (c + 1) + c] = held[q][glob[peer]]
            plane_copy(q, i).start()

        for s in range(c):
            picked[q][p * (c + 1) + s] = held[q][slots[p, s]]
        picked[q][p * (c + 1) + c] = held[q][glob[p]]

    def share(q):
        @pl.loop(1, PLANE)
        def _(i):
            plane_copy(q, i).wait_recv()

        relay[q] = picked[q][glob[PLANE + p] * (c + 1) + c]
        shared[q * PLANE + p] = relay[q]

        @pl.loop(1, PLANE)
        def _(i):
            shared_copy(q, i).start()

    fill(0)
    ring_start(0)
    fill(1)
    ring_start(1)
    for side in range(2):
        for kv in range(2):
            halo_copy(side, kv).start()
    fill(2)
    fill(3)
    ring((0, 1))
    ring_start(2)
    ring_start(3)
    spread(0)
    spread(1)
    ring((2, 3))
    spread(2)
    spread(3)
    for q in range(CHUNKS):
        share(q)
    for q in range(CHUNKS):

        @pl.loop(1, PLANE)
        def _(i):
            shared_copy(q, i).wait()
            plane_copy(q, i).wait_send()

        for d in range(2):
            for t in range(ring_hops(q, d)):
                ring_copy(q, d, t).wait_send()
    for side in range(2):
        for kv in range(2):
            halo_copy(side, kv).wait()


def fetch(c, slots, glob, key, value, collective_id):
    smem = pl.BlockSpec(memory_space=pltpu.SMEM)
    vmem = pl.BlockSpec(memory_space=pltpu.VMEM)
    part = jax.ShapeDtypeStruct((PLANE * (c + 1), ROWS, HEAD_DIM), BF16)
    dma = pltpu.SemaphoreType.DMA
    return pl.pallas_call(
        functools.partial(fetch_kernel, c),
        out_shape=(
            jax.ShapeDtypeStruct((4, BLOCK, WIDTH), BF16),
            jax.ShapeDtypeStruct((CHUNKS * PLANE, ROWS, HEAD_DIM), BF16),
        )
        + (part,) * CHUNKS,
        in_specs=[smem, smem, vmem, vmem],
        out_specs=(vmem,) * (2 + CHUNKS),
        scratch_shapes=[pltpu.VMEM((DEPTH * ITEMS, ROWS, HEAD_DIM), BF16)] * CHUNKS
        + [pltpu.VMEM(part.shape, BF16)] * CHUNKS
        + [
            pltpu.VMEM((CHUNKS, ROWS, HEAD_DIM), BF16),
            dma((7 * CHUNKS,)),
            dma((7 * CHUNKS,)),
            dma((CHUNKS * PLANE,)),
            dma((CHUNKS * PLANE,)),
            dma((CHUNKS * PLANE,)),
            dma((CHUNKS * PLANE,)),
            dma((4,)),
            dma((4,)),
        ],
        compiler_params=pltpu.CompilerParams(
            collective_id=collective_id, has_side_effects=True, vmem_limit_bytes=VMEM_BYTES
        ),
        name=f"fetch_{c}",
    )(slots, glob, key, value)


def dot(a, b, contract):
    return lax.dot_general(a, b, ((contract[0:1], contract[1:2]), ((), ())), preferred_element_type=F32)


def attend_kernel(
    where, query, grad, key, value, halo, shared, *rest
):
    picked = rest[0:4]
    attended, grad_query, own, sides, both = rest[4:9]
    terms = rest[9:13]
    seq = lax.axis_index("seq")
    scale = HEAD_DIM ** (-0.5)
    near = 4 * BLOCK
    rows = lax.broadcasted_iota(jnp.int32, (near, 128), 0)
    lanes = lax.broadcasted_iota(jnp.int32, (near, 128), 1)
    last = PLANE * DEPTH - 1
    first_block, second_block = lanes < BLOCK, lanes >= BLOCK
    hidden = (
        (first_block & (rows >= 3 * BLOCK))
        | (second_block & (rows < BLOCK))
        | ((rows < BLOCK) & (seq == 0))
        | ((rows >= 3 * BLOCK) & (seq == last))
    )
    pick_lanes = lax.broadcasted_iota(jnp.int32, (3 * BLOCK, 128), 1) < BLOCK

    @pl.loop(0, HEADS_HERE)
    def _(j):
        cols = pl.ds(pl.multiple_of(j * HEAD_DIM, HEAD_DIM), HEAD_DIM)
        q = query[:, cols]
        g = grad[:, cols]

        def listed(kv):
            near_part = [
                halo[kv, :, cols],
                (key, value)[kv][:, cols],
                halo[2 + kv, :, cols],
            ]
            for group in range(2):
                for half in range(2):
                    near_part.append(
                        shared[(kv * 2 + half) * PLANE + group * HEADS_HERE + j]
                    )
            far = []
            for b in range(BLOCKS_HERE):
                parts = []
                for t in range(3):
                    at = where[b * 24 + j * 3 + t]
                    for half in range(2):
                        parts.append(picked[kv * 2 + half][at])
                far.append(jnp.concatenate(parts, axis=0))
            return jnp.concatenate(near_part, axis=0), far

        keys, far_keys = listed(0)
        values, far_values = listed(1)

        def products(near_rows, far_rows, other):
            a = dot(near_rows, other, (1, 1))
            b = jnp.where(
                pick_lanes, dot(far_rows[0], other, (1, 1)), dot(far_rows[1], other, (1, 1))
            )
            return a, b

        s_near, s_far = products(keys, far_keys, q)
        s_near = s_near * scale
        s_far = s_far * scale
        s_near = jnp.concatenate(
            [jnp.where(hidden, -1e30, s_near[:near]), s_near[near:]], axis=0
        )
        top = jnp.maximum(
            jnp.max(s_near, axis=0, keepdims=True), jnp.max(s_far, axis=0, keepdims=True)
        )
        w_near = jnp.exp(s_near - top)
        w_far = jnp.exp(s_far - top)
        total = jnp.sum(w_near, axis=0, keepdims=True) + jnp.sum(w_far, axis=0, keepdims=True)
        inverse = 1.0 / total
        w_near = w_near * inverse
        w_far = w_far * inverse
        gw_near, gw_far = products(values, far_values, g)
        centre = jnp.sum(w_near * gw_near, axis=0, keepdims=True) + jnp.sum(
            w_far * gw_far, axis=0, keepdims=True
        )
        d_near = (w_near * (gw_near - centre) * scale).astype(BF16)
        d_far = (w_far * (gw_far - centre) * scale).astype(BF16)
        w_near = w_near.astype(BF16)
        w_far = w_far.astype(BF16)

        def gather(near_w, far_w, near_rows, far_rows):
            total_rows = dot(near_w, near_rows, (0, 0))
            top_rows = dot(far_w, far_rows[0], (0, 0))
            low_rows = dot(far_w, far_rows[1], (0, 0))
            return total_rows + jnp.concatenate([top_rows[:BLOCK], low_rows[BLOCK:]], axis=0)

        attended[:, cols] = gather(w_near, w_far, values, far_values).astype(BF16)
        grad_query[:, cols] = gather(d_near, d_far, keys, far_keys).astype(BF16)

        for kv in range(2):
            weight_near, weight_far = ((d_near, d_far), (w_near, w_far))[kv]
            rows_here = (q, g)[kv]
            near_terms = dot(weight_near, rows_here, (1, 0))
            zero = jnp.zeros_like(weight_far)
            for half in range(2):
                chunk = kv * 2 + half

                def piece(block):
                    return near_terms[block * BLOCK + half * ROWS : block * BLOCK + (half + 1) * ROWS]

                sides[chunk * HEADS_HERE + j] = piece(0).astype(BF16)
                sides[(CHUNKS + chunk) * HEADS_HERE + j] = piece(3).astype(BF16)
                for b in range(BLOCKS_HERE):
                    own[chunk * ITEMS + b * HEADS_HERE + j] = piece(1 + b)
                for group in range(2):
                    both[chunk * PLANE + group * HEADS_HERE + j] = piece(4 + group).astype(BF16)
            for b in range(BLOCKS_HERE):
                mine = jnp.where(pick_lanes, weight_far, zero) if b == 0 else jnp.where(
                    pick_lanes, zero, weight_far
                )
                far_terms = dot(mine, rows_here, (1, 0)).astype(BF16)
                for t in range(3):
                    for half in range(2):
                        start = t * BLOCK + half * ROWS
                        terms[kv * 2 + half][b * 24 + j * 3 + t] = far_terms[start : start + ROWS]


def attend(where, query, grad, key, value, halo, shared, picked):
    smem = pl.BlockSpec(memory_space=pltpu.SMEM)
    vmem = pl.BlockSpec(memory_space=pltpu.VMEM)
    rows = jax.ShapeDtypeStruct(query.shape, BF16)
    return pl.pallas_call(
        attend_kernel,
        out_shape=(
            rows,
            rows,
            jax.ShapeDtypeStruct((CHUNKS * ITEMS, ROWS, HEAD_DIM), F32),
            jax.ShapeDtypeStruct((2 * CHUNKS * HEADS_HERE, ROWS, HEAD_DIM), BF16),
            jax.ShapeDtypeStruct((CHUNKS * PLANE, ROWS, HEAD_DIM), BF16),
        )
        + (jax.ShapeDtypeStruct((PICKS, ROWS, HEAD_DIM), BF16),) * CHUNKS,
        in_specs=[smem] + [vmem] * (6 + CHUNKS),
        out_specs=(vmem,) * (5 + CHUNKS),
        compiler_params=pltpu.CompilerParams(vmem_limit_bytes=VMEM_BYTES),
        name="attend",
    )(where, query, grad, key, value, halo, shared, *picked)


def give_back_kernel(c, picks, order, first, ends, shared_ends, attended, grad_query, own, sides, both, *rest):
    terms, outs = rest[0:4], rest[4:8]
    out, arrived, totals, gathered = rest[8:12], rest[12:16], rest[16:20], rest[20:24]
    (
        relay, runs, zout, zin, beside, cross,
        zsend, zrecv, psend, precv, gsend, grecv, hsend, hrecv, csend, crecv,
    ) = rest[24:]
    seq, z, p, head = position()
    greet(z, p, seq, head, True)
    count = PLANE * c
    mine = pl.ds(pl.multiple_of(head * WIDTH, WIDTH), WIDTH)

    def result_copy(k):
        source = (attended, grad_query)[k].at[pl.ds((1 - head) * BLOCK, BLOCK)]
        return remote(source, outs[k].at[:, mine], csend.at[k], crecv.at[k], seq, 1 - head)

    def cross_copy(q):
        return remote(
            cross.at[q],
            outs[2 + q // 2].at[pl.ds((q % 2) * ROWS, ROWS), mine],
            csend.at[2 + q],
            crecv.at[2 + q],
            seq,
            1 - head,
        )

    def side_copy(side):
        size = CHUNKS * HEADS_HERE
        other = lax.rem(seq + (PLANE * DEPTH - 1 if side == 0 else 1), PLANE * DEPTH)
        return remote(
            sides.at[pl.ds(side * size, size)],
            beside.at[pl.ds((1 - side) * size, size)],
            hsend.at[side],
            hrecv.at[side],
            other,
            head,
        )

    def plane_copy(q, i):
        peer = lax.rem(p + i, PLANE)
        return remote(
            out[q].at[pl.ds(peer * (c + 1), c + 1)],
            arrived[q].at[pl.ds(p * (c + 1), c + 1)],
            psend.at[q * PLANE + i],
            precv.at[q * PLANE + i],
            z * PLANE + peer,
            head,
        )

    def shared_copy(q, i):
        peer = lax.rem(p + i, PLANE)
        return remote(
            relay.at[q],
            gathered[q].at[p],
            gsend.at[q * PLANE + i],
            grecv.at[q * PLANE + i],
            z * PLANE + peer,
            head,
        )

    def ring_copy(q, d, t):
        step = 1 if d == 0 else DEPTH - 1
        slot = ring_slot(q, d, t)
        return remote(
            zout.at[slot],
            zin.at[slot],
            zsend.at[slot],
            zrecv.at[slot],
            lax.rem(z + step, DEPTH) * PLANE + p,
            head,
        )

    def spread(q):
        @pl.loop(1, PLANE)
        def _(i):
            peer = lax.rem(p + i, PLANE)
            for s in range(c):
                out[q][peer * (c + 1) + s] = terms[q][picks[peer, s]]
            out[q][peer * (c + 1) + c] = both[q * PLANE + peer]
            plane_copy(q, i).start()

        for s in range(c):
            arrived[q][p * (c + 1) + s] = terms[q][picks[p, s]]
        arrived[q][p * (c + 1) + c] = both[q * PLANE + p]

    def share(q):
        @pl.loop(1, PLANE)
        def _(i):
            plane_copy(q, i).wait_recv()

        def add(i, total):
            return total + arrived[q][i * (c + 1) + c].astype(F32)

        total = lax.fori_loop(0, PLANE, add, jnp.zeros((ROWS, HEAD_DIM), F32))
        relay[q] = total.astype(BF16)
        gathered[q][p] = relay[q]
        gathered[q][PLANE] = jnp.zeros((ROWS, HEAD_DIM), BF16)

        @pl.loop(1, PLANE)
        def _(i):
            shared_copy(q, i).start()

    def collect(q):
        def add(r, total):
            term = arrived[q][order[r]].astype(F32)
            total = jnp.where(first[r] == 1, term, total + term)
            runs[r] = total
            return total

        lax.fori_loop(0, count, add, jnp.zeros((ROWS, HEAD_DIM), F32), unroll=4)

        @pl.loop(1, PLANE)
        def _(i):
            shared_copy(q, i).wait_recv()

        @pl.loop(0, DEPTH * ITEMS, unroll=4)
        def _(i):
            totals[q][i] = runs[ends[i]] + gathered[q][shared_ends[i]].astype(F32)

    def ring(chunks):
        for t in range(4):
            for q in chunks:
                for d in range(2):
                    hops = ring_hops(q, d)
                    if t < hops:
                        away = hops - t
                        target = lax.rem(z + (away if d == 0 else DEPTH - away), DEPTH)
                        rows = pl.ds(target * ITEMS, ITEMS)
                        partial = totals[q][rows]
                        if t > 0:
                            ring_copy(q, d, t - 1).wait_recv()
                            partial = partial + zin[ring_slot(q, d, t - 1)].astype(F32)
                        zout[ring_slot(q, d, t)] = partial.astype(BF16)
                        ring_copy(q, d, t).start()

    def finish(q):
        for d in range(2):
            ring_copy(q, d, ring_hops(q, d) - 1).wait_recv()
        kv, half = q // 2, q % 2
        for j in range(HEADS_HERE):
            for mine_too in range(2):
                b = head if mine_too else 1 - head
                item = b * HEADS_HERE + j
                total = totals[q][z * ITEMS + item] + own[q * ITEMS + item]
                total = total + beside[(b * CHUNKS + q) * HEADS_HERE + j].astype(F32)
                for d in range(2):
                    total = total + zin[ring_slot(q, d, ring_hops(q, d) - 1), item].astype(F32)
                total = total.astype(BF16)
                if mine_too:
                    cols = pl.ds(pl.multiple_of(head * WIDTH + j * HEAD_DIM, HEAD_DIM), HEAD_DIM)
                    outs[2 + kv][half * ROWS : (half + 1) * ROWS, cols] = total
                else:
                    cross[q, :, j * HEAD_DIM : (j + 1) * HEAD_DIM] = total
        cross_copy(q).start()

    for side in range(2):
        side_copy(side).start()
    for q in range(CHUNKS):
        spread(q)
    for k in range(2):
        result_copy(k).start()
        outs[k][:, mine] = (attended, grad_query)[k][pl.ds(pl.multiple_of(head * BLOCK, BLOCK), BLOCK)]
    runs[count] = jnp.zeros((ROWS, HEAD_DIM), F32)
    for q in range(CHUNKS):
        share(q)
    collect(0)
    collect(1)
    ring((0, 1))
    collect(2)
    collect(3)
    ring((2, 3))
    for side in range(2):
        side_copy(side).wait()
    for q in range(CHUNKS):
        finish(q)
    for q in range(CHUNKS):

        @pl.loop(1, PLANE)
        def _(i):
            shared_copy(q, i).wait_send()
            plane_copy(q, i).wait_send()

        for d in range(2):
            for t in range(ring_hops(q, d)):
                ring_copy(q, d, t).wait_send()
        cross_copy(q).wait()
    for k in range(2):
        result_copy(k).wait()


def give_back(c, picks, order, first, ends, shared_ends, attended, grad_query, own, sides, both, terms, collective_id):
    smem = pl.BlockSpec(memory_space=pltpu.SMEM)
    vmem = pl.BlockSpec(memory_space=pltpu.VMEM)
    dma = pltpu.SemaphoreType.DMA
    vm = pltpu.VMEM
    part = (PLANE * (c + 1), ROWS, HEAD_DIM)
    return pl.pallas_call(
        functools.partial(give_back_kernel, c),
        out_shape=(jax.ShapeDtypeStruct((BLOCK, 2 * WIDTH), BF16),) * 4,
        in_specs=[smem] * 5 + [vmem] * (5 + CHUNKS),
        out_specs=(vmem,) * 4,
        scratch_shapes=[vm(part, BF16)] * (2 * CHUNKS)
        + [vm((DEPTH * ITEMS, ROWS, HEAD_DIM), F32)] * CHUNKS
        + [vm((PLANE + 1, ROWS, HEAD_DIM), BF16)] * CHUNKS
        + [
            vm((CHUNKS, ROWS, HEAD_DIM), BF16),
            vm((PLANE * c + 1, ROWS, HEAD_DIM), F32),
            vm((7 * CHUNKS, ITEMS, ROWS, HEAD_DIM), BF16),
            vm((7 * CHUNKS, ITEMS, ROWS, HEAD_DIM), BF16),
            vm((2 * CHUNKS * HEADS_HERE, ROWS, HEAD_DIM), BF16),
            vm((CHUNKS, ROWS, WIDTH), BF16),
            dma((7 * CHUNKS,)),
            dma((7 * CHUNKS,)),
            dma((CHUNKS * PLANE,)),
            dma((CHUNKS * PLANE,)),
            dma((CHUNKS * PLANE,)),
            dma((CHUNKS * PLANE,)),
            dma((2,)),
            dma((2,)),
            dma((2 + CHUNKS,)),
            dma((2 + CHUNKS,)),
        ],
        compiler_params=pltpu.CompilerParams(
            collective_id=collective_id, has_side_effects=True, vmem_limit_bytes=VMEM_BYTES
        ),
        name=f"give_back_{c}",
    )(picks, order, first, ends, shared_ends, attended, grad_query, own, sides, both, *terms)


def on_device(
    query_vectors, key_vectors, value_vectors, cotangent, rand_peer, rand_local, global_ids
):
    seq = lax.axis_index("seq")
    column = seq % PLANE
    none = DEPTH * ITEMS
    peers = rand_peer[0].reshape(PICKS)
    heads = jnp.arange(HEADS_HERE, dtype=jnp.int32)
    inner = (rand_local[0] * HEADS_HERE + heads[None, :, None]).reshape(PICKS)
    items = (peers // PLANE) * ITEMS + inner
    columns = peers % PLANE
    numbers = jnp.arange(PICKS, dtype=jnp.int32)
    earlier = (columns[:, None] == columns[None, :]) & (numbers[None, :] < numbers[:, None])
    ranks = jnp.sum(earlier.astype(jnp.int32), axis=1)
    spots = columns * PLANE + ranks
    hits = spots[None, :] == jnp.arange(PLANE * PLANE, dtype=jnp.int32)[:, None]
    table = jnp.min(jnp.where(hits, items[None, :], none), axis=1).reshape(PLANE, PLANE)
    picks = jnp.max(jnp.where(hits, numbers[None, :], 0), axis=1).reshape(PLANE, PLANE)
    most = jnp.max(ranks) + 1
    lanes = jnp.arange(128, dtype=jnp.int32)
    padded = jnp.pad(table, ((0, 0), (0, 128 - PLANE)), constant_values=0)
    padded = jnp.where(lanes[None, :] == PLANE, most, padded)
    got, peaks = swap_tables(jnp.broadcast_to(padded[:, None, :], (PLANE, 8, 128)))
    asked = got[:, 0, :PLANE]
    peak = jnp.max(peaks[:, 0, PLANE])
    last_block = PLANE * DEPTH * BLOCKS_HERE - 1
    pair = jnp.stack([global_ids[0] + global_ids[1] - last_block, jnp.array(last_block, jnp.int32)])
    pair_peer = pair // BLOCKS_HERE
    pair_items = (pair_peer // PLANE) * ITEMS + (pair % BLOCKS_HERE) * HEADS_HERE
    pair_items = (pair_items[:, None] + heads[None, :]).reshape(PLANE)
    pair_columns = jnp.repeat(pair_peer % PLANE, HEADS_HERE)
    glob = jnp.concatenate([pair_items, pair_columns])
    all_items = jnp.arange(none, dtype=jnp.int32)
    here = (pair_items[None, :] == all_items[:, None]) & (pair_columns[None, :] == column)
    shared_ends = jnp.min(
        jnp.where(here, jnp.arange(PLANE, dtype=jnp.int32)[None, :], PLANE), axis=1
    )

    def path(c, ids):
        def run(query, key, value, grad):
            wanted = asked[:, :c]
            slots = jnp.where(wanted == none, 0, wanted)
            halo, shared, *picked = fetch(c, slots, glob, key, value, ids[0])
            where = columns * (c + 1) + ranks
            attended, grad_query, own, sides, both, *terms = attend(
                where, query, grad, key, value, halo, shared, picked
            )
            count = PLANE * c
            keys = wanted.reshape(count)
            at = jnp.arange(count, dtype=jnp.int32)
            before = (keys[None, :] < keys[:, None]) | (
                (keys[None, :] == keys[:, None]) & (at[None, :] < at[:, None])
            )
            sorted_at = jnp.sum(before.astype(jnp.int32), axis=1)
            chosen = sorted_at[None, :] == at[:, None]
            spot = (at // c) * (c + 1) + at % c
            order = jnp.sum(jnp.where(chosen, spot[None, :], 0), axis=1)
            opens = ~jnp.any((keys[None, :] == keys[:, None]) & (at[None, :] < at[:, None]), axis=1)
            first = jnp.sum(jnp.where(chosen & opens[None, :], 1, 0), axis=1)
            upto = jnp.sum((keys[None, :] <= all_items[:, None]).astype(jnp.int32), axis=1)
            found = jnp.any(keys[None, :] == all_items[:, None], axis=1)
            ends = jnp.where(found, upto - 1, count)
            return give_back(
                c, picks[:, :c], order, first, ends, shared_ends,
                attended, grad_query, own, sides, both, terms, ids[1],
            )

        return run

    return lax.cond(
        peak > 8, path(16, (3, 4)), path(8, (1, 2)),
        query_vectors, key_vectors, value_vectors, cotangent,
    )


def solution(mesh):
    placed = (
        P("seq", "head"),
        P("seq", "head"),
        P("seq", "head"),
        P("seq", "head"),
        P("head", "seq", None, None),
        P("head", "seq", None, None),
        P(),
    )
    return jax.shard_map(
        on_device,
        mesh=mesh,
        in_specs=placed,
        out_specs=(P(("seq", "head"), None),) * 4,
        check_vma=False,
    )
```

```python
import functools

import jax
import jax.numpy as jnp
from jax import lax
from jax.experimental import pallas as pl
from jax.experimental.pallas import tpu as pltpu
from jax.sharding import PartitionSpec as P

MESH = pl.DeviceIdType.MESH
HEAD_DIM = 128
BLOCK = 64
HEADS_HERE = 8
BLOCKS_HERE = 2
WIDTH = HEADS_HERE * HEAD_DIM
PLANE = 16
DEPTH = 8
ITEMS = BLOCKS_HERE * HEADS_HERE
PICKS = 3 * ITEMS
ROWS = 16
PARTS = BLOCK // ROWS
CHUNKS = 2 * PARTS
LANES = 32
FULL = PLANE + 1
USUAL = 8
VMEM_BYTES = 56 * 1024 * 1024
F32 = jnp.float32
BF16 = jnp.bfloat16


def position():
    seq = lax.axis_index("seq")
    return seq, lax.div(seq, PLANE), lax.rem(seq, PLANE), lax.axis_index("head")


def signal(seq, head):
    pl.semaphore_signal(
        pltpu.get_barrier_semaphore(), inc=1, device_id=(seq, head), device_id_type=MESH
    )


def remote(src, dst, send, recv, seq, head):
    return pltpu.make_async_remote_copy(
        src_ref=src,
        dst_ref=dst,
        send_sem=send,
        recv_sem=recv,
        device_id=(seq, head),
        device_id_type=MESH,
    )


def ring_hops(q, d):
    return 4 if (d == 0) == (q % 2 == 0) else 3


def ring_slot(q, d, t):
    return sum(ring_hops(q, e) for e in range(d)) + 7 * q + t


def fetch_kernel(c, glob, table, key, value, got, most, halo, shared, *rest):
    picked, held, out = rest[0:CHUNKS], rest[CHUNKS : 2 * CHUNKS], rest[2 * CHUNKS : 3 * CHUNKS]
    (
        relay, slots, local,
        zsend, zrecv, psend, precv, gsend, grecv, hsend, hrecv, tsend, trecv, msend, mrecv,
    ) = rest[3 * CHUNKS :]
    seq, z, p, head = position()
    place = z * 2 + head

    def table_copy(i):
        peer = lax.rem(p + i, PLANE)
        return remote(
            table.at[peer], got.at[p], tsend.at[i], trecv.at[i], z * PLANE + peer, head
        )

    def most_copy(i):
        other = lax.rem(place + i, 2 * DEPTH)
        return remote(
            most.at[place],
            most.at[place],
            msend.at[i],
            mrecv.at[i],
            lax.div(other, 2) * PLANE + p,
            lax.rem(other, 2),
        )

    def halo_copy(side, kv):
        block = (1 - side) * BLOCK
        other = lax.rem(seq + (1 if side == 0 else PLANE * DEPTH - 1), PLANE * DEPTH)
        return remote(
            (key, value)[kv].at[pl.ds(block, BLOCK)],
            halo.at[side * 2 + kv],
            hsend.at[side * 2 + kv],
            hrecv.at[side * 2 + kv],
            other,
            head,
        )

    def ring_copy(q, d, t):
        step = 1 if d == 0 else DEPTH - 1
        owner = lax.rem(z + t * (DEPTH - step), DEPTH)
        rows = pl.ds(owner * ITEMS, ITEMS)
        slot = ring_slot(q, d, t)
        return remote(
            held[q].at[rows],
            held[q].at[rows],
            zsend.at[slot],
            zrecv.at[slot],
            lax.rem(z + step, DEPTH) * PLANE + p,
            head,
        )

    def plane_copy(q, i):
        peer = lax.rem(p + i, PLANE)
        return remote(
            out[q].at[pl.ds(peer * c, c)],
            picked[q].at[pl.ds(p * c, c)],
            psend.at[q * PLANE + i],
            precv.at[q * PLANE + i],
            z * PLANE + peer,
            head,
        )

    def shared_copy(q, i):
        peer = lax.rem(p + i, PLANE)
        return remote(
            relay.at[q],
            shared.at[q * PLANE + p],
            gsend.at[q * PLANE + i],
            grecv.at[q * PLANE + i],
            z * PLANE + peer,
            head,
        )

    def fill(q):
        source, part = (key, value)[q // PARTS], q % PARTS
        for b in range(BLOCKS_HERE):
            for j in range(HEADS_HERE):
                held[q][z * ITEMS + b * HEADS_HERE + j] = source[
                    b * BLOCK + part * ROWS : b * BLOCK + (part + 1) * ROWS,
                    j * HEAD_DIM : (j + 1) * HEAD_DIM,
                ]

    def ring_start(q):
        for d in range(2):
            ring_copy(q, d, 0).start()

    def ring_step(q, t):
        for d in range(2):
            if t < ring_hops(q, d):
                ring_copy(q, d, t).wait_recv()
                if t + 1 < ring_hops(q, d):
                    ring_copy(q, d, t + 1).start()

    def spread(q):
        @pl.loop(1, PLANE)
        def _(i):
            peer = lax.rem(p + i, PLANE)
            for s in range(c):
                out[q][peer * c + s] = held[q][slots[peer, 0, s]]
            plane_copy(q, i).start()

        for s in range(c):
            picked[q][p * c + s] = held[q][slots[p, 0, s]]

    def share(q):
        @pl.loop(1, PLANE)
        def _(i):
            plane_copy(q, i).wait_recv()

        relay[q] = picked[q][glob[0]]
        shared[q * PLANE + p] = relay[q]

        @pl.loop(1, PLANE)
        def _(i):
            shared_copy(q, i).start()

    fill(0)

    @pl.loop(1, 2 * DEPTH)
    def _(i):
        other = lax.rem(place + i, 2 * DEPTH)
        signal(lax.div(other, 2) * PLANE + p, lax.rem(other, 2))

    @pl.loop(1, PLANE)
    def _(i):
        signal(z * PLANE + lax.rem(p + i, PLANE), head)

    for step in (1, PLANE * DEPTH - 1):
        signal(lax.rem(seq + step, PLANE * DEPTH), head)
    pl.semaphore_wait(pltpu.get_barrier_semaphore(), 2 * DEPTH - 1 + PLANE - 1 + 2)

    ring_start(0)

    @pl.loop(1, PLANE)
    def _(i):
        table_copy(i).start()

    got[p] = table[p]
    for q in range(1, CHUNKS):
        fill(q)
    for side in range(2):
        for kv in range(2):
            halo_copy(side, kv).start()

    ring_start(1)
    for step in range(CHUNKS + 4):
        for t in range(3, -1, -1):
            if 0 <= step - t < CHUNKS:
                ring_step(step - t, t)
        if step + 2 < CHUNKS:
            ring_start(step + 2)
        if step == 2:

            @pl.loop(1, PLANE)
            def _(i):
                table_copy(i).wait()

            to_scalars = pltpu.make_async_copy(got, slots, local)
            to_scalars.start()
            to_scalars.wait()
        if 0 <= step - 3 < CHUNKS:
            spread(step - 3)
        if step == 4:
            most[place] = jnp.max(got[...], axis=0)

            @pl.loop(1, 2 * DEPTH)
            def _(i):
                most_copy(i).start()

    for q in range(CHUNKS):
        share(q)

    @pl.loop(1, 2 * DEPTH)
    def _(i):
        most_copy(i).wait()

    for q in range(CHUNKS):

        @pl.loop(1, PLANE)
        def _(i):
            shared_copy(q, i).wait()
            plane_copy(q, i).wait_send()

        for d in range(2):
            for t in range(ring_hops(q, d)):
                ring_copy(q, d, t).wait_send()
    for side in range(2):
        for kv in range(2):
            halo_copy(side, kv).wait()


def fetch(c, glob, table, key, value, collective_id):
    smem = pl.BlockSpec(memory_space=pltpu.SMEM)
    vmem = pl.BlockSpec(memory_space=pltpu.VMEM)
    part = jax.ShapeDtypeStruct((PLANE * c, ROWS, HEAD_DIM), BF16)
    rows = jax.ShapeDtypeStruct((PLANE, 8, 128), jnp.int32)
    dma = pltpu.SemaphoreType.DMA
    return pl.pallas_call(
        functools.partial(fetch_kernel, c),
        out_shape=(
            rows,
            rows,
            jax.ShapeDtypeStruct((4, BLOCK, WIDTH), BF16),
            jax.ShapeDtypeStruct((CHUNKS * PLANE, ROWS, HEAD_DIM), BF16),
        )
        + (part,) * CHUNKS,
        in_specs=[smem, vmem, vmem, vmem],
        out_specs=(vmem,) * (4 + CHUNKS),
        scratch_shapes=[pltpu.VMEM((DEPTH * ITEMS, ROWS, HEAD_DIM), BF16)] * CHUNKS
        + [pltpu.VMEM(part.shape, BF16)] * CHUNKS
        + [
            pltpu.VMEM((CHUNKS, ROWS, HEAD_DIM), BF16),
            pltpu.SMEM((PLANE, 8, 128), jnp.int32),
            dma(()),
            dma((7 * CHUNKS,)),
            dma((7 * CHUNKS,)),
            dma((CHUNKS * PLANE,)),
            dma((CHUNKS * PLANE,)),
            dma((CHUNKS * PLANE,)),
            dma((CHUNKS * PLANE,)),
            dma((4,)),
            dma((4,)),
            dma((PLANE,)),
            dma((PLANE,)),
            dma((2 * DEPTH,)),
            dma((2 * DEPTH,)),
        ],
        compiler_params=pltpu.CompilerParams(
            collective_id=collective_id, has_side_effects=True, vmem_limit_bytes=VMEM_BYTES
        ),
        name=f"fetch_{c}",
    )(glob, table, key, value)


def dot(a, b, contract):
    return lax.dot_general(a, b, ((contract[0:1], contract[1:2]), ((), ())), preferred_element_type=F32)


def back_kernel(c, where, picks, order, first, ends, shared_ends, query, grad, key, value, halo, shared, *rest):
    picked, rest = rest[:CHUNKS], rest[CHUNKS:]
    outs, rest = rest[:4], rest[4:]
    terms, rest = rest[:CHUNKS], rest[CHUNKS:]
    out, rest = rest[:CHUNKS], rest[CHUNKS:]
    arrived, rest = rest[:CHUNKS], rest[CHUNKS:]
    totals, rest = rest[:CHUNKS], rest[CHUNKS:]
    gathered, rest = rest[:CHUNKS], rest[CHUNKS:]
    (
        attended, grad_query, own, sides, both, weights,
        relay, runs, zout, zin, beside, cross,
        zsend, zrecv, psend, precv, gsend, grecv, hsend, hrecv, csend, crecv,
    ) = rest
    seq, z, p, head = position()

    @pl.loop(1, PLANE)
    def _(i):
        signal(z * PLANE + lax.rem(p + i, PLANE), head)

    for step in (1, DEPTH - 1):
        signal(lax.rem(z + step, DEPTH) * PLANE + p, head)
    for step in (1, PLANE * DEPTH - 1):
        signal(lax.rem(seq + step, PLANE * DEPTH), head)
    signal(seq, 1 - head)

    scale = HEAD_DIM ** (-0.5)
    near = 4 * BLOCK
    rows = lax.broadcasted_iota(jnp.int32, (near, 128), 0)
    lanes = lax.broadcasted_iota(jnp.int32, (near, 128), 1)
    hidden = (
        ((lanes < BLOCK) & (rows >= 3 * BLOCK))
        | ((lanes >= BLOCK) & (rows < BLOCK))
        | ((rows < BLOCK) & (seq == 0))
        | ((rows >= 3 * BLOCK) & (seq == PLANE * DEPTH - 1))
    )
    pick_lanes = lax.broadcasted_iota(jnp.int32, (3 * BLOCK, 128), 1) < BLOCK

    def columns_of(j):
        return pl.ds(pl.multiple_of(j * HEAD_DIM, HEAD_DIM), HEAD_DIM)

    def listed(kv, j):
        cols = columns_of(j)
        close = [halo[kv, :, cols], (key, value)[kv][:, cols], halo[2 + kv, :, cols]]
        for group in range(2):
            for part in range(PARTS):
                close.append(shared[(kv * PARTS + part) * PLANE + group * HEADS_HERE + j])
        far = []
        for b in range(BLOCKS_HERE):
            pieces = []
            for t in range(3):
                at = where[b * 24 + j * 3 + t]
                for part in range(PARTS):
                    pieces.append(picked[kv * PARTS + part][at])
            far.append(jnp.concatenate(pieces, axis=0))
        return jnp.concatenate(close, axis=0), far

    def products(close, far, other):
        a = dot(close, other, (1, 1))
        b = jnp.where(pick_lanes, dot(far[0], other, (1, 1)), dot(far[1], other, (1, 1)))
        return a, b

    def gather(near_w, far_w, close, far):
        total = dot(near_w, close, (0, 0))
        top_rows = dot(far_w, far[0], (0, 0))
        low_rows = dot(far_w, far[1], (0, 0))
        return total + jnp.concatenate([top_rows[:BLOCK], low_rows[BLOCK:]], axis=0)

    def scatter(kv, j, weight_near, weight_far, rows_here):
        near_terms = dot(weight_near, rows_here, (1, 0))
        zero = jnp.zeros_like(weight_far)
        far_terms = (
            dot(jnp.where(pick_lanes, weight_far, zero), rows_here, (1, 0)).astype(BF16),
            dot(jnp.where(pick_lanes, zero, weight_far), rows_here, (1, 0)).astype(BF16),
        )
        for part in range(PARTS):
            chunk = kv * PARTS + part

            def piece(block):
                start = block * BLOCK + part * ROWS
                return near_terms[start : start + ROWS]

            sides[chunk * HEADS_HERE + j] = piece(0).astype(BF16)
            sides[(CHUNKS + chunk) * HEADS_HERE + j] = piece(3).astype(BF16)
            for b in range(BLOCKS_HERE):
                own[chunk * ITEMS + b * HEADS_HERE + j] = piece(1 + b)
                for t in range(3):
                    start = t * BLOCK + part * ROWS
                    terms[chunk][b * 24 + j * 3 + t] = far_terms[b][start : start + ROWS]
            for group in range(2):
                both[chunk * PLANE + group * HEADS_HERE + j] = piece(4 + group).astype(BF16)

    def weigh(j):
        cols = columns_of(j)
        keys, far_keys = listed(0, j)
        s_near, s_far = products(keys, far_keys, query[:, cols])
        s_near = s_near * scale
        s_far = s_far * scale
        s_near = jnp.concatenate(
            [jnp.where(hidden, -1e30, s_near[:near]), s_near[near:]], axis=0
        )
        top = jnp.maximum(
            jnp.max(s_near, axis=0, keepdims=True), jnp.max(s_far, axis=0, keepdims=True)
        )
        w_near = jnp.exp(s_near - top)
        w_far = jnp.exp(s_far - top)
        total = jnp.sum(w_near, axis=0, keepdims=True) + jnp.sum(w_far, axis=0, keepdims=True)
        inverse = 1.0 / total
        w_near = w_near * inverse
        w_far = w_far * inverse
        weights[j, : 6 * BLOCK] = w_near
        weights[j, 6 * BLOCK :] = w_far
        scatter(1, j, w_near.astype(BF16), w_far.astype(BF16), grad[:, cols])

    def backward(j):
        cols = columns_of(j)
        q, g = query[:, cols], grad[:, cols]
        keys, far_keys = listed(0, j)
        values, far_values = listed(1, j)
        w_near, w_far = weights[j, : 6 * BLOCK], weights[j, 6 * BLOCK :]
        gw_near, gw_far = products(values, far_values, g)
        centre = jnp.sum(w_near * gw_near, axis=0, keepdims=True) + jnp.sum(
            w_far * gw_far, axis=0, keepdims=True
        )
        d_near = (w_near * (gw_near - centre) * scale).astype(BF16)
        d_far = (w_far * (gw_far - centre) * scale).astype(BF16)
        scatter(0, j, d_near, d_far, q)
        attended[:, cols] = gather(
            w_near.astype(BF16), w_far.astype(BF16), values, far_values
        ).astype(BF16)
        grad_query[:, cols] = gather(d_near, d_far, keys, far_keys).astype(BF16)

    count = PLANE * c
    mine = pl.ds(pl.multiple_of(head * WIDTH, WIDTH), WIDTH)

    def result_copy(k):
        source = (attended, grad_query)[k].at[pl.ds((1 - head) * BLOCK, BLOCK)]
        return remote(source, outs[k].at[:, mine], csend.at[k], crecv.at[k], seq, 1 - head)

    def cross_copy(q):
        return remote(
            cross.at[q],
            outs[2 + q // PARTS].at[pl.ds((q % PARTS) * ROWS, ROWS), mine],
            csend.at[2 + q],
            crecv.at[2 + q],
            seq,
            1 - head,
        )

    def side_copy(kv, side):
        size = PARTS * HEADS_HERE
        other = lax.rem(seq + (PLANE * DEPTH - 1 if side == 0 else 1), PLANE * DEPTH)
        return remote(
            sides.at[pl.ds((side * 2 + kv) * size, size)],
            beside.at[pl.ds(((1 - side) * 2 + kv) * size, size)],
            hsend.at[kv * 2 + side],
            hrecv.at[kv * 2 + side],
            other,
            head,
        )

    def plane_copy(q, i):
        peer = lax.rem(p + i, PLANE)
        return remote(
            out[q].at[pl.ds(peer * (c + 1), c + 1)],
            arrived[q].at[pl.ds(p * (c + 1), c + 1)],
            psend.at[q * PLANE + i],
            precv.at[q * PLANE + i],
            z * PLANE + peer,
            head,
        )

    def shared_copy(q, i):
        peer = lax.rem(p + i, PLANE)
        return remote(
            relay.at[q],
            gathered[q].at[p],
            gsend.at[q * PLANE + i],
            grecv.at[q * PLANE + i],
            z * PLANE + peer,
            head,
        )

    def shared_out(i):
        return (p < HEADS_HERE) | (lax.rem(p + i, PLANE) == PLANE - 1)

    def shared_in(i):
        return (lax.rem(p + PLANE - i, PLANE) < HEADS_HERE) | (p == PLANE - 1)

    def ring_copy(q, d, t):
        step = 1 if d == 0 else DEPTH - 1
        slot = ring_slot(q, d, t)
        return remote(
            zout.at[slot],
            zin.at[slot],
            zsend.at[slot],
            zrecv.at[slot],
            lax.rem(z + step, DEPTH) * PLANE + p,
            head,
        )

    def spread(q):
        @pl.loop(1, PLANE)
        def _(i):
            peer = lax.rem(p + i, PLANE)
            for s in range(c):
                out[q][peer * (c + 1) + s] = terms[q][picks[peer, s]]
            out[q][peer * (c + 1) + c] = both[q * PLANE + peer]
            plane_copy(q, i).start()

        for s in range(c):
            arrived[q][p * (c + 1) + s] = terms[q][picks[p, s]]
        arrived[q][p * (c + 1) + c] = both[q * PLANE + p]

    def share(q):
        @pl.loop(1, PLANE)
        def _(i):
            plane_copy(q, i).wait_recv()

        total = arrived[q][c].astype(F32)
        for i in range(1, PLANE):
            total = total + arrived[q][i * (c + 1) + c].astype(F32)
        relay[q] = total.astype(BF16)
        gathered[q][p] = relay[q]
        gathered[q][PLANE] = jnp.zeros((ROWS, HEAD_DIM), BF16)

        @pl.loop(1, PLANE)
        def _(i):
            @pl.when(shared_out(i))
            def _():
                shared_copy(q, i).start()

    def collect(q):
        def add(r, total):
            term = arrived[q][order[r]].astype(F32)
            total = jnp.where(first[r] == 1, term, total + term)
            runs[r] = total
            return total

        lax.fori_loop(0, count, add, jnp.zeros((ROWS, HEAD_DIM), F32), unroll=8)

        @pl.loop(1, PLANE)
        def _(i):
            @pl.when(shared_in(i))
            def _():
                shared_copy(q, i).wait_recv()

        @pl.loop(0, DEPTH * ITEMS, unroll=8)
        def _(i):
            totals[q][i] = runs[ends[i]] + gathered[q][shared_ends[i]].astype(F32)

    def ring_step(q, t):
        for d in range(2):
            hops = ring_hops(q, d)
            if t < hops:
                away = hops - t
                target = lax.rem(z + (away if d == 0 else DEPTH - away), DEPTH)
                partial = totals[q][pl.ds(target * ITEMS, ITEMS)]
                if t > 0:
                    ring_copy(q, d, t - 1).wait_recv()
                    partial = partial + zin[ring_slot(q, d, t - 1)].astype(F32)
                zout[ring_slot(q, d, t)] = partial.astype(BF16)
                ring_copy(q, d, t).start()

    def finish(q):
        for d in range(2):
            ring_copy(q, d, ring_hops(q, d) - 1).wait_recv()
        kv, part = q // PARTS, q % PARTS
        for j in range(HEADS_HERE):
            for stays in range(2):
                b = head if stays else 1 - head
                item = b * HEADS_HERE + j
                total = totals[q][z * ITEMS + item] + own[q * ITEMS + item]
                total = total + beside[(b * CHUNKS + q) * HEADS_HERE + j].astype(F32)
                for d in range(2):
                    total = total + zin[ring_slot(q, d, ring_hops(q, d) - 1), item].astype(F32)
                total = total.astype(BF16)
                if stays:
                    cols = pl.ds(pl.multiple_of(head * WIDTH + j * HEAD_DIM, HEAD_DIM), HEAD_DIM)
                    outs[2 + kv][part * ROWS : (part + 1) * ROWS, cols] = total
                else:
                    cross[q, :, j * HEAD_DIM : (j + 1) * HEAD_DIM] = total
        cross_copy(q).start()

    @pl.loop(0, HEADS_HERE)
    def _(j):
        weigh(j)

    runs[count] = jnp.zeros((ROWS, HEAD_DIM), F32)
    pl.semaphore_wait(pltpu.get_barrier_semaphore(), PLANE + 4)
    turn = list(range(PARTS, CHUNKS)) + list(range(PARTS))
    spread(turn[0])
    spread(turn[1])
    for side in range(2):
        side_copy(1, side).start()

    @pl.loop(0, HEADS_HERE)
    def _(j):
        backward(j)

    for k in range(2):
        result_copy(k).start()
        outs[k][:, mine] = (attended, grad_query)[k][pl.ds(pl.multiple_of(head * BLOCK, BLOCK), BLOCK)]
    for side in range(2):
        side_copy(0, side).start()
    for step in range(CHUNKS + 6):
        if step + 2 < CHUNKS:
            spread(turn[step + 2])
        for t in range(3, 0, -1):
            if 0 <= step - 1 - t < CHUNKS:
                ring_step(turn[step - 1 - t], t)
        if 0 <= step - 1 < CHUNKS:
            collect(turn[step - 1])
            ring_step(turn[step - 1], 0)
        if step < CHUNKS:
            share(turn[step])
        if 0 <= step - 5 < CHUNKS:
            q = turn[step - 5]
            if q % PARTS == 0:
                for side in range(2):
                    side_copy(q // PARTS, side).wait()
            finish(q)
    for q in range(CHUNKS):

        @pl.loop(1, PLANE)
        def _(i):
            @pl.when(shared_out(i))
            def _():
                shared_copy(q, i).wait_send()

            plane_copy(q, i).wait_send()

        for d in range(2):
            for t in range(ring_hops(q, d)):
                ring_copy(q, d, t).wait_send()
        cross_copy(q).wait()
    for k in range(2):
        result_copy(k).wait()


def back(c, scalars, arrays, picked, collective_id):
    smem = pl.BlockSpec(memory_space=pltpu.SMEM)
    vmem = pl.BlockSpec(memory_space=pltpu.VMEM)
    dma = pltpu.SemaphoreType.DMA
    vm = pltpu.VMEM
    tile = (ROWS, HEAD_DIM)
    part = (PLANE * (c + 1),) + tile
    return pl.pallas_call(
        functools.partial(back_kernel, c),
        out_shape=(jax.ShapeDtypeStruct((BLOCK, 2 * WIDTH), BF16),) * 4,
        in_specs=[smem] * len(scalars) + [vmem] * (len(arrays) + CHUNKS),
        out_specs=(vmem,) * 4,
        scratch_shapes=[vm((PICKS,) + tile, BF16)] * CHUNKS
        + [vm(part, BF16)] * (2 * CHUNKS)
        + [vm((DEPTH * ITEMS,) + tile, F32)] * CHUNKS
        + [vm((PLANE + 1,) + tile, BF16)] * CHUNKS
        + [
            vm((BLOCKS_HERE * BLOCK, WIDTH), BF16),
            vm((BLOCKS_HERE * BLOCK, WIDTH), BF16),
            vm((CHUNKS * ITEMS,) + tile, F32),
            vm((2 * CHUNKS * HEADS_HERE,) + tile, BF16),
            vm((CHUNKS * PLANE,) + tile, BF16),
            vm((HEADS_HERE, 9 * BLOCK, 128), F32),
            vm((CHUNKS,) + tile, BF16),
            vm((PLANE * c + 1,) + tile, F32),
            vm((7 * CHUNKS, ITEMS) + tile, BF16),
            vm((7 * CHUNKS, ITEMS) + tile, BF16),
            vm((2 * CHUNKS * HEADS_HERE,) + tile, BF16),
            vm((CHUNKS, ROWS, WIDTH), BF16),
            dma((7 * CHUNKS,)),
            dma((7 * CHUNKS,)),
            dma((CHUNKS * PLANE,)),
            dma((CHUNKS * PLANE,)),
            dma((CHUNKS * PLANE,)),
            dma((CHUNKS * PLANE,)),
            dma((4,)),
            dma((4,)),
            dma((2 + CHUNKS,)),
            dma((2 + CHUNKS,)),
        ],
        compiler_params=pltpu.CompilerParams(
            collective_id=collective_id, has_side_effects=True, vmem_limit_bytes=VMEM_BYTES
        ),
        name=f"back_{c}",
    )(*scalars, *arrays, *picked)


def on_device(
    query_vectors, key_vectors, value_vectors, cotangent, rand_peer, rand_local, global_ids
):
    seq = lax.axis_index("seq")
    column = seq % PLANE
    none = DEPTH * ITEMS
    heads = jnp.arange(HEADS_HERE, dtype=jnp.int32)
    last_block = PLANE * DEPTH * BLOCKS_HERE - 1
    pair = jnp.stack([global_ids[0] + global_ids[1] - last_block, jnp.array(last_block, jnp.int32)])
    pair_peer = pair // BLOCKS_HERE
    pair_items = (pair_peer // PLANE) * ITEMS + (pair % BLOCKS_HERE) * HEADS_HERE
    pair_items = (pair_items[:, None] + heads[None, :]).reshape(PLANE)
    pair_columns = jnp.repeat(pair_peer % PLANE, HEADS_HERE)
    peers = rand_peer[0].reshape(PICKS)
    inner = (rand_local[0] * HEADS_HERE + heads[None, :, None]).reshape(PICKS)
    items = (peers // PLANE) * ITEMS + inner
    relayed = jnp.arange(PLANE, dtype=jnp.int32) == column
    relay_item = jnp.sum(jnp.where(relayed, pair_items, 0))
    relay_column = jnp.sum(jnp.where(relayed, pair_columns, 0))
    items = jnp.concatenate([items, relay_item[None]])
    columns = jnp.concatenate([peers % PLANE, relay_column[None]])
    numbers = jnp.arange(PICKS + 1, dtype=jnp.int32)
    earlier = (columns[:, None] == columns[None, :]) & (numbers[None, :] < numbers[:, None])
    ranks = jnp.sum(earlier.astype(jnp.int32), axis=1)
    spots = columns * LANES + ranks
    hits = spots[None, :] == jnp.arange(PLANE * LANES, dtype=jnp.int32)[:, None]
    back_hits = hits & (numbers[None, :] < PICKS)
    table = jnp.max(jnp.where(hits, items[None, :], 0), axis=1).reshape(PLANE, LANES)
    back_keys = jnp.min(jnp.where(back_hits, items[None, :], none), axis=1).reshape(PLANE, LANES)
    picks = jnp.max(jnp.where(back_hits, numbers[None, :], 0), axis=1).reshape(PLANE, LANES)
    most = jnp.broadcast_to(jnp.max(ranks) + 1, (PLANE, LANES))
    padded = jnp.concatenate(
        [table, most, back_keys, jnp.zeros((PLANE, 128 - 3 * LANES), jnp.int32)], axis=1
    )
    padded = jnp.broadcast_to(padded[:, None, :], (PLANE, 8, 128))
    all_items = jnp.arange(none, dtype=jnp.int32)
    here = (pair_items[None, :] == all_items[:, None]) & (pair_columns[None, :] == column)
    shared_ends = jnp.min(
        jnp.where(here, jnp.arange(PLANE, dtype=jnp.int32)[None, :], PLANE), axis=1
    )

    def go(c, collective_id, key, value):
        at = jnp.minimum(relay_column * c + ranks[PICKS], PLANE * c - 1)[None]
        return fetch(c, at, padded, key, value, collective_id)

    def finish(c, collective_id, query, key, value, grad, fetched):
        got, _, halo, shared, *picked = fetched
        where = columns * c + ranks
        count = PLANE * c
        keys = got[:, 0, 2 * LANES : 2 * LANES + c].reshape(count)
        at = jnp.arange(count, dtype=jnp.int32)
        same = keys[None, :] == keys[:, None]
        ahead = at[None, :] < at[:, None]
        before = (keys[None, :] < keys[:, None]) | (same & ahead)
        sorted_at = jnp.sum(before.astype(jnp.int32), axis=1)
        chosen = sorted_at[None, :] == at[:, None]
        spot = (at // c) * (c + 1) + at % c
        order = jnp.sum(jnp.where(chosen, spot[None, :], 0), axis=1)
        opens = ~jnp.any(same & ahead, axis=1)
        first = jnp.sum(jnp.where(chosen & opens[None, :], 1, 0), axis=1)
        upto = jnp.sum((keys[None, :] <= all_items[:, None]).astype(jnp.int32), axis=1)
        found = jnp.any(keys[None, :] == all_items[:, None], axis=1)
        ends = jnp.where(found, upto - 1, count)
        return back(
            c,
            (where, picks[:, :c], order, first, ends, shared_ends),
            (query, grad, key, value, halo, shared),
            picked,
            collective_id,
        )

    def usual(query, key, value, grad, *fetched):
        return finish(USUAL, 1, query, key, value, grad, fetched)

    def crowded(query, key, value, grad, *fetched):
        return finish(FULL, 3, query, key, value, grad, go(FULL, 2, key, value))

    fetched = go(USUAL, 0, key_vectors, value_vectors)
    peak = jnp.max(fetched[1][:, 0, LANES])
    return lax.cond(
        peak > USUAL, crowded, usual,
        query_vectors, key_vectors, value_vectors, cotangent, *fetched,
    )


def solution(mesh):
    placed = (
        P("seq", "head"),
        P("seq", "head"),
        P("seq", "head"),
        P("seq", "head"),
        P("head", "seq", None, None),
        P("head", "seq", None, None),
        P(),
    )
    return jax.shard_map(
        on_device,
        mesh=mesh,
        in_specs=placed,
        out_specs=(P(("seq", "head"), None),) * 4,
        check_vma=False,
    )
```

```python
import functools

import jax
import jax.numpy as jnp
from jax import lax
from jax.experimental import pallas as pl
from jax.experimental.pallas import tpu as pltpu
from jax.sharding import PartitionSpec as P

MESH = pl.DeviceIdType.MESH
HEAD_DIM = 128
BLOCK = 64
HEADS_HERE = 8
BLOCKS_HERE = 2
WIDTH = HEADS_HERE * HEAD_DIM
PLANE = 16
DEPTH = 8
ITEMS = BLOCKS_HERE * HEADS_HERE
PICKS = 3 * ITEMS
ROWS = 16
PARTS = BLOCK // ROWS
CHUNKS = 2 * PARTS
LANES = 32
FULL = 2 * DEPTH
USUAL = 8
LAST_BLOCK = PLANE * DEPTH * BLOCKS_HERE - 1
VMEM_BYTES = 56 * 1024 * 1024
F32 = jnp.float32
BF16 = jnp.bfloat16


def position():
    seq = lax.axis_index("seq")
    return seq, lax.div(seq, PLANE), lax.rem(seq, PLANE), lax.axis_index("head")


def signal(seq, head):
    pl.semaphore_signal(
        pltpu.get_barrier_semaphore(), inc=1, device_id=(seq, head), device_id_type=MESH
    )


def remote(src, dst, send, recv, seq, head):
    return pltpu.make_async_remote_copy(
        src_ref=src,
        dst_ref=dst,
        send_sem=send,
        recv_sem=recv,
        device_id=(seq, head),
        device_id_type=MESH,
    )


def ring_hops(q, d):
    return 4 if (d == 0) == (q % 2 == 0) else 3


def ring_slot(q, d, t):
    return sum(ring_hops(q, e) for e in range(d)) + 7 * q + t


def global_block(ids, e):
    return jnp.where(e < HEADS_HERE, ids[0] + ids[1] - LAST_BLOCK, LAST_BLOCK)


def global_place(ids, e):
    block = global_block(ids, e)
    peer = block >> 1
    plane = peer >> 4
    item = plane * ITEMS + (block & 1) * HEADS_HERE + lax.rem(e, HEADS_HERE)
    return plane, peer & (PLANE - 1), item


def write_tables(c, rand_peer, rand_local, table, where, plan):
    shape = (PICKS, 128)
    number = lax.broadcasted_iota(jnp.int32, shape, 0)
    lane = lax.broadcasted_iota(jnp.int32, shape, 1)

    def spread_out(ref):
        parts = []
        for t in range(3):
            for b in range(BLOCKS_HERE):
                parts.append(jnp.broadcast_to(ref[0, b][:, t : t + 1], (HEADS_HERE, 128)))
        return jnp.concatenate(parts, axis=0)

    peer, spot = spread_out(rand_peer), spread_out(rand_local)
    column = peer & (PLANE - 1)
    item = (peer >> 4) * ITEMS + spot * HEADS_HERE + (number & (HEADS_HERE - 1))
    along = jnp.sum(jnp.where(number == lane, column, 0), axis=0, keepdims=True)
    ahead = (column == along) & (lane < number)
    rank = jnp.sum(jnp.where(ahead, 1, 0), axis=1, keepdims=True)
    rank = jnp.broadcast_to(rank, shape)
    most = jnp.max(rank, axis=0, keepdims=True) + 1
    where[...] = jnp.minimum(column * c + rank, PLANE * c - 1)
    group = lane >> 5
    none = DEPTH * ITEMS
    worth = jnp.where(group == 0, item, 0)
    worth = jnp.where(group == 2, item - none, worth)
    worth = jnp.where(group == 3, number, worth)
    here = rank == (lane & (LANES - 1))
    row_group = group[0:1]
    rest = jnp.where(row_group == 2, none, jnp.where(row_group == 1, most, 0))
    for col in range(PLANE):
        line = jnp.sum(jnp.where(here & (column == col), worth, 0), axis=0, keepdims=True)
        line = line + rest
        table[col] = jnp.broadcast_to(line, (8, 128))
        plan[col : col + 1, :] = line


def fetch_kernel(c, ids, rand_peer, rand_local, key, value, got, peak, where, plan, halo, shared, *rest):
    picked, held, out = rest[0:CHUNKS], rest[CHUNKS : 2 * CHUNKS] + (shared,), rest[2 * CHUNKS : 3 * CHUNKS]
    (
        relay, offer, offered, piece, pieces, slots, table, most, local,
        zsend, zrecv, psend, precv, gsend, grecv, hsend, hrecv, tsend, trecv, msend, mrecv,
    ) = rest[3 * CHUNKS :]
    seq, z, p, head = position()
    place = z * 2 + head

    def table_copy(i):
        peer = lax.rem(p + i, PLANE)
        return remote(
            table.at[peer], got.at[p], tsend.at[i], trecv.at[i], z * PLANE + peer, head
        )

    def most_copy(i):
        other = lax.rem(place + i, 2 * DEPTH)
        return remote(
            most.at[place],
            most.at[place],
            msend.at[i],
            mrecv.at[i],
            lax.div(other, 2) * PLANE + p,
            lax.rem(other, 2),
        )

    def halo_copy(side, kv):
        block = (1 - side) * BLOCK
        other = lax.rem(seq + (1 if side == 0 else PLANE * DEPTH - 1), PLANE * DEPTH)
        return remote(
            (key, value)[kv].at[pl.ds(block, BLOCK)],
            halo.at[side * 2 + kv],
            hsend.at[side * 2 + kv],
            hrecv.at[side * 2 + kv],
            other,
            head,
        )

    def ring_copy(q, d, t):
        step = 1 if d == 0 else DEPTH - 1
        owner = lax.rem(z + t * (DEPTH - step), DEPTH)
        rows = pl.ds(owner * ITEMS, ITEMS)
        slot = ring_slot(q, d, t)
        return remote(
            held[q].at[rows],
            held[q].at[rows],
            zsend.at[slot],
            zrecv.at[slot],
            lax.rem(z + step, DEPTH) * PLANE + p,
            head,
        )

    def plane_copy(q, i):
        peer = lax.rem(p + i, PLANE)
        return remote(
            out[q].at[pl.ds(peer * c, c)],
            picked[q].at[pl.ds(p * c, c)],
            psend.at[q * PLANE + i],
            precv.at[q * PLANE + i],
            z * PLANE + peer,
            head,
        )

    def offer_copy(i):
        peer = lax.rem(p + i, PLANE)
        return remote(
            offer.at[pl.ds(peer * CHUNKS, CHUNKS)],
            offered.at[pl.ds(p * CHUNKS, CHUNKS)],
            gsend.at[i],
            grecv.at[i],
            z * PLANE + peer,
            head,
        )

    def piece_copy(i):
        other = lax.rem(z + i, DEPTH)
        return remote(
            piece.at[other],
            pieces.at[z],
            gsend.at[PLANE + i],
            grecv.at[PLANE + i],
            other * PLANE + p,
            head,
        )

    def relay_copy(i):
        return remote(
            relay,
            shared.at[z * PLANE + p],
            gsend.at[PLANE + DEPTH + i],
            grecv.at[PLANE + DEPTH + i],
            z * PLANE + lax.rem(p + i, PLANE),
            head,
        )

    def offers(sender, peer):
        return (peer < HEADS_HERE) | (sender == PLANE - 1)

    def offer_start():
        for e in range(PLANE):
            second = (global_block(ids, e) & 1) == 1
            j = e % HEADS_HERE
            for q in range(CHUNKS):
                low, high = [
                    (key, value)[q // PARTS][
                        b * BLOCK + (q % PARTS) * ROWS : b * BLOCK + (q % PARTS + 1) * ROWS,
                        j * HEAD_DIM : (j + 1) * HEAD_DIM,
                    ]
                    for b in range(BLOCKS_HERE)
                ]
                offer[e * CHUNKS + q] = jnp.where(second, high, low)

        @pl.loop(1, PLANE)
        def _(i):
            @pl.when(offers(p, lax.rem(p + i, PLANE)))
            def _():
                offer_copy(i).start()

        mine = pl.ds(p * CHUNKS, CHUNKS)
        offered[mine] = offer[mine]

    def piece_start():
        @pl.loop(1, PLANE)
        def _(i):
            @pl.when(offers(lax.rem(p + PLANE - i, PLANE), p))
            def _():
                offer_copy(i).wait_recv()

        _, column, _ = global_place(ids, p)
        for q in range(CHUNKS):
            found = offered[(PLANE - 1) * CHUNKS + q]
            for source in range(PLANE - 1):
                found = jnp.where(column == source, offered[source * CHUNKS + q], found)
            piece[q] = found

        @pl.loop(1, DEPTH)
        def _(i):
            piece_copy(i).start()

        pieces[z] = piece[z]

    def relay_start():
        @pl.loop(1, DEPTH)
        def _(i):
            piece_copy(i).wait_recv()

        plane, _, _ = global_place(ids, p)
        found = pieces[DEPTH - 1]
        for source in range(DEPTH - 1):
            found = jnp.where(plane == source, pieces[source], found)
        relay[...] = found
        shared[z * PLANE + p] = relay[...]

        @pl.loop(1, PLANE)
        def _(i):
            relay_copy(i).start()

    def relay_wait():
        @pl.loop(1, PLANE)
        def _(i):
            relay_copy(i).wait_recv()

    def fill(q):
        source, part = (key, value)[q // PARTS], q % PARTS
        for b in range(BLOCKS_HERE):
            for j in range(HEADS_HERE):
                held[q][z * ITEMS + b * HEADS_HERE + j] = source[
                    b * BLOCK + part * ROWS : b * BLOCK + (part + 1) * ROWS,
                    j * HEAD_DIM : (j + 1) * HEAD_DIM,
                ]

    def ring_start(q):
        for d in range(2):
            ring_copy(q, d, 0).start()

    def ring_step(q, t):
        for d in range(2):
            if t < ring_hops(q, d):
                ring_copy(q, d, t).wait_recv()
                if t + 1 < ring_hops(q, d):
                    ring_copy(q, d, t + 1).start()

    def spread(q):
        @pl.loop(1, PLANE)
        def _(i):
            peer = lax.rem(p + i, PLANE)
            for s in range(c):
                out[q][peer * c + s] = held[q][slots[peer, 0, s]]
            plane_copy(q, i).start()

        for s in range(c):
            picked[q][p * c + s] = held[q][slots[p, 0, s]]

    fill(0)

    @pl.loop(1, 2 * DEPTH)
    def _(i):
        other = lax.rem(place + i, 2 * DEPTH)
        signal(lax.div(other, 2) * PLANE + p, lax.rem(other, 2))

    @pl.loop(1, PLANE)
    def _(i):
        signal(z * PLANE + lax.rem(p + i, PLANE), head)

    for step in (1, PLANE * DEPTH - 1):
        signal(lax.rem(seq + step, PLANE * DEPTH), head)
    pl.semaphore_wait(pltpu.get_barrier_semaphore(), 2 * DEPTH - 1 + PLANE - 1 + 2)

    ring_start(0)
    fill(1)
    ring_start(1)
    write_tables(c, rand_peer, rand_local, table, where, plan)

    @pl.loop(1, PLANE)
    def _(i):
        table_copy(i).start()

    got[p] = table[p]
    offer_start()
    for q in range(2, CHUNKS):
        fill(q)
    for side in range(2):
        for kv in range(2):
            halo_copy(side, kv).start()

    for step in range(CHUNKS + 4):
        for t in range(3, -1, -1):
            if 0 <= step - t <= CHUNKS:
                ring_step(step - t, t)
        if step + 2 == CHUNKS:
            relay_wait()
        if step + 2 <= CHUNKS:
            ring_start(step + 2)
        if step == 1:
            piece_start()
        if step == 3:
            relay_start()
        if step == 2:

            @pl.loop(1, PLANE)
            def _(i):
                table_copy(i).wait()

            to_scalars = pltpu.make_async_copy(got, slots, local)
            to_scalars.start()
            to_scalars.wait()
        if 0 <= step - 3 < CHUNKS:
            spread(step - 3)
        if step == 4:
            most[place] = jnp.max(got[...], axis=0)

            @pl.loop(1, 2 * DEPTH)
            def _(i):
                most_copy(i).start()

    @pl.loop(1, 2 * DEPTH)
    def _(i):
        most_copy(i).wait()

    peak[...] = jnp.max(most[...], axis=0)
    @pl.loop(1, PLANE)
    def _(i):
        @pl.when(offers(p, lax.rem(p + i, PLANE)))
        def _():
            offer_copy(i).wait_send()

        relay_copy(i).wait_send()

    @pl.loop(1, DEPTH)
    def _(i):
        piece_copy(i).wait_send()

    for q in range(CHUNKS + 1):
        if q < CHUNKS:

            @pl.loop(1, PLANE)
            def _(i):
                plane_copy(q, i).wait()

        for d in range(2):
            for t in range(ring_hops(q, d)):
                ring_copy(q, d, t).wait_send()
    for side in range(2):
        for kv in range(2):
            halo_copy(side, kv).wait()


def fetch(c, ids, rand_peer, rand_local, key, value, collective_id):
    smem = pl.BlockSpec(memory_space=pltpu.SMEM)
    vmem = pl.BlockSpec(memory_space=pltpu.VMEM)
    part = jax.ShapeDtypeStruct((PLANE * c, ROWS, HEAD_DIM), BF16)
    rows = jax.ShapeDtypeStruct((PLANE, 8, 128), jnp.int32)
    dma = pltpu.SemaphoreType.DMA
    return pl.pallas_call(
        functools.partial(fetch_kernel, c),
        out_shape=(
            rows,
            jax.ShapeDtypeStruct((8, 128), jnp.int32),
            jax.ShapeDtypeStruct((PICKS, 128), jnp.int32),
            jax.ShapeDtypeStruct((PLANE, 128), jnp.int32),
            jax.ShapeDtypeStruct((4, BLOCK, WIDTH), BF16),
            jax.ShapeDtypeStruct((CHUNKS * PLANE, ROWS, HEAD_DIM), BF16),
        )
        + (part,) * CHUNKS,
        in_specs=[smem, vmem, vmem, vmem, vmem],
        out_specs=(vmem,) * (6 + CHUNKS),
        scratch_shapes=[pltpu.VMEM((DEPTH * ITEMS, ROWS, HEAD_DIM), BF16)] * CHUNKS
        + [pltpu.VMEM(part.shape, BF16)] * CHUNKS
        + [
            pltpu.VMEM((ROWS, HEAD_DIM), BF16),
            pltpu.VMEM((PLANE * CHUNKS, ROWS, HEAD_DIM), BF16),
            pltpu.VMEM((PLANE * CHUNKS, ROWS, HEAD_DIM), BF16),
            pltpu.VMEM((DEPTH, ROWS, HEAD_DIM), BF16),
            pltpu.VMEM((DEPTH, ROWS, HEAD_DIM), BF16),
            pltpu.SMEM((PLANE, 8, 128), jnp.int32),
            pltpu.VMEM((PLANE, 8, 128), jnp.int32),
            pltpu.VMEM((2 * DEPTH, 8, 128), jnp.int32),
            dma(()),
            dma((7 * (CHUNKS + 1),)),
            dma((7 * (CHUNKS + 1),)),
            dma((CHUNKS * PLANE,)),
            dma((CHUNKS * PLANE,)),
            dma((2 * PLANE + DEPTH,)),
            dma((2 * PLANE + DEPTH,)),
            dma((4,)),
            dma((4,)),
            dma((PLANE,)),
            dma((PLANE,)),
            dma((2 * DEPTH,)),
            dma((2 * DEPTH,)),
        ],
        compiler_params=pltpu.CompilerParams(
            collective_id=collective_id, has_side_effects=True, vmem_limit_bytes=VMEM_BYTES
        ),
        name=f"fetch_{c}",
    )(ids, rand_peer, rand_local, key, value)


def dot(a, b, contract):
    return lax.dot_general(a, b, ((contract[0:1], contract[1:2]), ((), ())), preferred_element_type=F32)


def back_kernel(c, ids, where, plan, order, first, ends, query, grad, key, value, halo, shared, *rest):
    picked, rest = rest[:CHUNKS], rest[CHUNKS:]
    outs, rest = rest[:4], rest[4:]
    terms, rest = rest[:CHUNKS], rest[CHUNKS:]
    out, rest = rest[:CHUNKS], rest[CHUNKS:]
    arrived, rest = rest[:CHUNKS], rest[CHUNKS:]
    totals, rest = rest[:CHUNKS], rest[CHUNKS:]
    (
        attended, grad_query, own, sides, both, weights,
        zone_in, zone, tile_in, tile_total, relay, runs, zout, zin, beside, cross,
        zsend, zrecv, psend, precv, gsend, grecv, hsend, hrecv, csend, crecv,
    ) = rest
    seq, z, p, head = position()

    @pl.loop(1, PLANE)
    def _(i):
        signal(z * PLANE + lax.rem(p + i, PLANE), head)

    @pl.loop(1, DEPTH)
    def _(i):
        signal(lax.rem(z + i, DEPTH) * PLANE + p, head)

    for step in (1, PLANE * DEPTH - 1):
        signal(lax.rem(seq + step, PLANE * DEPTH), head)
    signal(seq, 1 - head)

    scale = HEAD_DIM ** (-0.5)
    near = 4 * BLOCK
    rows = lax.broadcasted_iota(jnp.int32, (near, 128), 0)
    lanes = lax.broadcasted_iota(jnp.int32, (near, 128), 1)
    hidden = (
        ((lanes < BLOCK) & (rows >= 3 * BLOCK))
        | ((lanes >= BLOCK) & (rows < BLOCK))
        | ((rows < BLOCK) & (seq == 0))
        | ((rows >= 3 * BLOCK) & (seq == PLANE * DEPTH - 1))
    )
    pick_lanes = lax.broadcasted_iota(jnp.int32, (3 * BLOCK, 128), 1) < BLOCK

    def columns_of(j):
        return pl.ds(pl.multiple_of(j * HEAD_DIM, HEAD_DIM), HEAD_DIM)

    def listed(kv, j):
        cols = columns_of(j)
        close = [halo[kv, :, cols], (key, value)[kv][:, cols], halo[2 + kv, :, cols]]
        for group in range(2):
            for part in range(PARTS):
                close.append(shared[(kv * PARTS + part) * PLANE + group * HEADS_HERE + j])
        far = []
        for b in range(BLOCKS_HERE):
            pieces = []
            for t in range(3):
                at = where[t * ITEMS + b * HEADS_HERE + j, 0]
                for part in range(PARTS):
                    pieces.append(picked[kv * PARTS + part][at])
            far.append(jnp.concatenate(pieces, axis=0))
        return jnp.concatenate(close, axis=0), far

    def products(close, far, other):
        a = dot(close, other, (1, 1))
        b = jnp.where(pick_lanes, dot(far[0], other, (1, 1)), dot(far[1], other, (1, 1)))
        return a, b

    def gather(near_w, far_w, close, far):
        total = dot(near_w, close, (0, 0))
        top_rows = dot(far_w, far[0], (0, 0))
        low_rows = dot(far_w, far[1], (0, 0))
        return total + jnp.concatenate([top_rows[:BLOCK], low_rows[BLOCK:]], axis=0)

    def scatter(kv, j, weight_near, weight_far, rows_here):
        near_terms = dot(weight_near, rows_here, (1, 0))
        zero = jnp.zeros_like(weight_far)
        far_terms = (
            dot(jnp.where(pick_lanes, weight_far, zero), rows_here, (1, 0)).astype(BF16),
            dot(jnp.where(pick_lanes, zero, weight_far), rows_here, (1, 0)).astype(BF16),
        )
        for part in range(PARTS):
            chunk = kv * PARTS + part

            def piece(block):
                start = block * BLOCK + part * ROWS
                return near_terms[start : start + ROWS]

            sides[chunk * HEADS_HERE + j] = piece(0).astype(BF16)
            sides[(CHUNKS + chunk) * HEADS_HERE + j] = piece(3).astype(BF16)
            for b in range(BLOCKS_HERE):
                own[chunk * ITEMS + b * HEADS_HERE + j] = piece(1 + b)
                for t in range(3):
                    start = t * BLOCK + part * ROWS
                    terms[chunk][t * ITEMS + b * HEADS_HERE + j] = far_terms[b][start : start + ROWS]
            for group in range(2):
                both[((kv * 2 + group) * HEADS_HERE + j) * PARTS + part] = piece(4 + group).astype(BF16)

    def weigh(j):
        cols = columns_of(j)
        keys, far_keys = listed(0, j)
        s_near, s_far = products(keys, far_keys, query[:, cols])
        s_near = s_near * scale
        s_far = s_far * scale
        s_near = jnp.concatenate(
            [jnp.where(hidden, -1e30, s_near[:near]), s_near[near:]], axis=0
        )
        top = jnp.maximum(
            jnp.max(s_near, axis=0, keepdims=True), jnp.max(s_far, axis=0, keepdims=True)
        )
        w_near = jnp.exp(s_near - top)
        w_far = jnp.exp(s_far - top)
        total = jnp.sum(w_near, axis=0, keepdims=True) + jnp.sum(w_far, axis=0, keepdims=True)
        inverse = 1.0 / total
        w_near = w_near * inverse
        w_far = w_far * inverse
        weights[j, : 6 * BLOCK] = w_near
        weights[j, 6 * BLOCK :] = w_far
        scatter(1, j, w_near.astype(BF16), w_far.astype(BF16), grad[:, cols])

    def backward(j):
        cols = columns_of(j)
        q, g = query[:, cols], grad[:, cols]
        keys, far_keys = listed(0, j)
        values, far_values = listed(1, j)
        w_near, w_far = weights[j, : 6 * BLOCK], weights[j, 6 * BLOCK :]
        gw_near, gw_far = products(values, far_values, g)
        centre = jnp.sum(w_near * gw_near, axis=0, keepdims=True) + jnp.sum(
            w_far * gw_far, axis=0, keepdims=True
        )
        d_near = (w_near * (gw_near - centre) * scale).astype(BF16)
        d_far = (w_far * (gw_far - centre) * scale).astype(BF16)
        scatter(0, j, d_near, d_far, q)
        attended[:, cols] = gather(
            w_near.astype(BF16), w_far.astype(BF16), values, far_values
        ).astype(BF16)
        grad_query[:, cols] = gather(d_near, d_far, keys, far_keys).astype(BF16)

    count = PLANE * c
    mine = pl.ds(pl.multiple_of(head * WIDTH, WIDTH), WIDTH)

    def result_copy(k):
        source = (attended, grad_query)[k].at[pl.ds((1 - head) * BLOCK, BLOCK)]
        return remote(source, outs[k].at[:, mine], csend.at[k], crecv.at[k], seq, 1 - head)

    def cross_copy(q):
        return remote(
            cross.at[q],
            outs[2 + q // PARTS].at[pl.ds((q % PARTS) * ROWS, ROWS), mine],
            csend.at[2 + q],
            crecv.at[2 + q],
            seq,
            1 - head,
        )

    def side_copy(kv, side):
        size = PARTS * HEADS_HERE
        other = lax.rem(seq + (PLANE * DEPTH - 1 if side == 0 else 1), PLANE * DEPTH)
        return remote(
            sides.at[pl.ds((side * 2 + kv) * size, size)],
            beside.at[pl.ds(((1 - side) * 2 + kv) * size, size)],
            hsend.at[kv * 2 + side],
            hrecv.at[kv * 2 + side],
            other,
            head,
        )

    def plane_copy(q, i):
        peer = lax.rem(p + i, PLANE)
        return remote(
            out[q].at[pl.ds(peer * c, c)],
            arrived[q].at[pl.ds(p * c, c)],
            psend.at[q * PLANE + i],
            precv.at[q * PLANE + i],
            z * PLANE + peer,
            head,
        )

    def zone_copy(kv, i):
        other = lax.rem(z + i, DEPTH)
        rows = pl.ds((kv * PLANE + other * 2) * PARTS, 2 * PARTS)
        return remote(
            both.at[rows],
            zone_in.at[pl.ds((kv * DEPTH + z) * 2 * PARTS, 2 * PARTS)],
            gsend.at[kv * DEPTH + i],
            grecv.at[kv * DEPTH + i],
            other * PLANE + p,
            head,
        )

    def tile_copy(kv, i):
        peer = lax.rem(p + i, PLANE)
        return remote(
            zone.at[kv * 2 * PARTS + lax.rem(peer, 2 * PARTS)],
            tile_in.at[p],
            gsend.at[2 * DEPTH + i],
            grecv.at[2 * DEPTH + i],
            z * PLANE + peer,
            head,
        )

    def total_copy(i):
        peer = lax.rem(p + i, PLANE)
        return remote(
            relay,
            tile_total.at[p],
            gsend.at[2 * DEPTH + PLANE + i],
            grecv.at[2 * DEPTH + PLANE + i],
            z * PLANE + peer,
            head,
        )

    def adds(kv, q):
        return lax.div(q, 2 * PARTS) == 1 - kv

    def zone_start(kv):
        @pl.loop(1, DEPTH)
        def _(i):
            zone_copy(kv, i).start()

    def zone_add(kv):
        @pl.loop(1, DEPTH)
        def _(i):
            zone_copy(kv, i).wait_recv()

        size = 2 * PARTS
        total = both[pl.ds((kv * PLANE + z * 2) * PARTS, size)].astype(F32)
        for i in range(1, DEPTH):
            other = lax.rem(z + i, DEPTH)
            total = total + zone_in[pl.ds((kv * DEPTH + other) * size, size)].astype(F32)
        zone[kv * size : (kv + 1) * size] = total.astype(BF16)

        @pl.loop(1, PLANE)
        def _(i):
            @pl.when(adds(kv, lax.rem(p + i, PLANE)))
            def _():
                tile_copy(kv, i).start()

    def tile_add(kv):
        @pl.when(adds(kv, p))
        def _():
            @pl.loop(1, PLANE)
            def _(i):
                tile_copy(kv, i).wait_recv()

            tile_in[p] = zone[kv * 2 * PARTS + lax.rem(p, 2 * PARTS)]
            total = tile_in[0].astype(F32)
            for i in range(1, PLANE):
                total = total + tile_in[i].astype(F32)
            relay[...] = total.astype(BF16)
            tile_total[p] = relay[...]

            @pl.loop(1, PLANE)
            def _(i):
                total_copy(i).start()

    def total_wait(kv):
        @pl.loop(1, PLANE)
        def _(i):
            @pl.when(adds(kv, lax.rem(p + PLANE - i, PLANE)))
            def _():
                total_copy(i).wait_recv()

    def ring_copy(q, d, t):
        step = 1 if d == 0 else DEPTH - 1
        slot = ring_slot(q, d, t)
        return remote(
            zout.at[slot],
            zin.at[slot],
            zsend.at[slot],
            zrecv.at[slot],
            lax.rem(z + step, DEPTH) * PLANE + p,
            head,
        )

    def spread(q):
        @pl.loop(1, PLANE)
        def _(i):
            peer = lax.rem(p + i, PLANE)
            for s in range(c):
                out[q][peer * c + s] = terms[q][plan[peer, 3 * LANES + s]]
            plane_copy(q, i).start()

        for s in range(c):
            arrived[q][p * c + s] = terms[q][plan[p, 3 * LANES + s]]

    def collect(q):
        @pl.loop(1, PLANE)
        def _(i):
            plane_copy(q, i).wait_recv()

        def add(r, total):
            term = arrived[q][order[r]].astype(F32)
            total = jnp.where(first[r] == 1, term, total + term)
            runs[r] = total
            return total

        lax.fori_loop(0, count, add, jnp.zeros((ROWS, HEAD_DIM), F32), unroll=8)
        kv, part = q // PARTS, q % PARTS
        if part == 0:
            total_wait(kv)
        extra = [
            tile_total[(1 - kv) * 2 * PARTS + e * PARTS + part].astype(F32) for e in range(2)
        ]
        spots = []
        for e in range(2):
            _, column, item = global_place(ids, z * 2 + e)
            spots.append(jnp.where(column == p, item, -1))

        @pl.loop(0, DEPTH * ITEMS, unroll=8)
        def _(i):
            total = runs[ends[i]]
            for e in range(2):
                total = total + jnp.where(spots[e] == i, extra[e], 0.0)
            totals[q][i] = total

    def ring_step(q, t):
        for d in range(2):
            hops = ring_hops(q, d)
            if t < hops:
                away = hops - t
                target = lax.rem(z + (away if d == 0 else DEPTH - away), DEPTH)
                partial = totals[q][pl.ds(target * ITEMS, ITEMS)]
                if t > 0:
                    ring_copy(q, d, t - 1).wait_recv()
                    partial = partial + zin[ring_slot(q, d, t - 1)].astype(F32)
                zout[ring_slot(q, d, t)] = partial.astype(BF16)
                ring_copy(q, d, t).start()

    def finish(q):
        for d in range(2):
            ring_copy(q, d, ring_hops(q, d) - 1).wait_recv()
        kv, part = q // PARTS, q % PARTS
        for j in range(HEADS_HERE):
            for stays in range(2):
                b = head if stays else 1 - head
                item = b * HEADS_HERE + j
                total = totals[q][z * ITEMS + item] + own[q * ITEMS + item]
                total = total + beside[(b * CHUNKS + q) * HEADS_HERE + j].astype(F32)
                for d in range(2):
                    total = total + zin[ring_slot(q, d, ring_hops(q, d) - 1), item].astype(F32)
                total = total.astype(BF16)
                if stays:
                    cols = pl.ds(pl.multiple_of(head * WIDTH + j * HEAD_DIM, HEAD_DIM), HEAD_DIM)
                    outs[2 + kv][part * ROWS : (part + 1) * ROWS, cols] = total
                else:
                    cross[q, :, j * HEAD_DIM : (j + 1) * HEAD_DIM] = total
        cross_copy(q).start()

    @pl.loop(0, HEADS_HERE)
    def _(j):
        weigh(j)

    runs[count] = jnp.zeros((ROWS, HEAD_DIM), F32)
    pl.semaphore_wait(pltpu.get_barrier_semaphore(), PLANE + DEPTH + 1)
    turn = list(range(PARTS, CHUNKS)) + list(range(PARTS))
    zone_start(1)
    for side in range(2):
        side_copy(1, side).start()
    spread(turn[0])
    spread(turn[1])

    @pl.loop(0, HEADS_HERE)
    def _(j):
        backward(j)

    zone_add(1)
    spread(turn[2])
    zone_start(0)
    for side in range(2):
        side_copy(0, side).start()
    for k in range(2):
        result_copy(k).start()
        outs[k][:, mine] = (attended, grad_query)[k][pl.ds(pl.multiple_of(head * BLOCK, BLOCK), BLOCK)]
    for step in range(CHUNKS + 5):
        if 0 < step and step + 2 < CHUNKS:
            spread(turn[step + 2])
        if step == 0:
            tile_add(1)
        if step == 1:
            zone_add(0)
        if step == 3:
            tile_add(0)
        for t in range(3, 0, -1):
            if 0 <= step - t < CHUNKS:
                ring_step(turn[step - t], t)
        if step < CHUNKS:
            collect(turn[step])
            ring_step(turn[step], 0)
        if 0 <= step - 4 < CHUNKS:
            q = turn[step - 4]
            if q % PARTS == 0:
                for side in range(2):
                    side_copy(q // PARTS, side).wait()
            finish(q)
    for kv in range(2):

        @pl.loop(1, DEPTH)
        def _(i):
            zone_copy(kv, i).wait_send()

        @pl.loop(1, PLANE)
        def _(i):
            @pl.when(adds(kv, lax.rem(p + i, PLANE)))
            def _():
                tile_copy(kv, i).wait_send()

    @pl.loop(1, PLANE)
    def _(i):
        total_copy(i).wait_send()

    for q in range(CHUNKS):

        @pl.loop(1, PLANE)
        def _(i):
            plane_copy(q, i).wait_send()

        for d in range(2):
            for t in range(ring_hops(q, d)):
                ring_copy(q, d, t).wait_send()
        cross_copy(q).wait()
    for k in range(2):
        result_copy(k).wait()


def back(c, scalars, arrays, picked, collective_id):
    smem = pl.BlockSpec(memory_space=pltpu.SMEM)
    vmem = pl.BlockSpec(memory_space=pltpu.VMEM)
    dma = pltpu.SemaphoreType.DMA
    vm = pltpu.VMEM
    tile = (ROWS, HEAD_DIM)
    part = (PLANE * c,) + tile
    return pl.pallas_call(
        functools.partial(back_kernel, c),
        out_shape=(jax.ShapeDtypeStruct((BLOCK, 2 * WIDTH), BF16),) * 4,
        in_specs=[smem] * len(scalars) + [vmem] * (len(arrays) + CHUNKS),
        out_specs=(vmem,) * 4,
        scratch_shapes=[vm((PICKS,) + tile, BF16)] * CHUNKS
        + [vm(part, BF16)] * (2 * CHUNKS)
        + [vm((DEPTH * ITEMS,) + tile, F32)] * CHUNKS
        + [
            vm((BLOCKS_HERE * BLOCK, WIDTH), BF16),
            vm((BLOCKS_HERE * BLOCK, WIDTH), BF16),
            vm((CHUNKS * ITEMS,) + tile, F32),
            vm((2 * CHUNKS * HEADS_HERE,) + tile, BF16),
            vm((CHUNKS * PLANE,) + tile, BF16),
            vm((HEADS_HERE, 9 * BLOCK, 128), F32),
            vm((2 * DEPTH * 2 * PARTS,) + tile, BF16),
            vm((2 * 2 * PARTS,) + tile, BF16),
            vm((PLANE,) + tile, BF16),
            vm((PLANE,) + tile, BF16),
            vm(tile, BF16),
            vm((PLANE * c + 1,) + tile, F32),
            vm((7 * CHUNKS, ITEMS) + tile, BF16),
            vm((7 * CHUNKS, ITEMS) + tile, BF16),
            vm((2 * CHUNKS * HEADS_HERE,) + tile, BF16),
            vm((CHUNKS, ROWS, WIDTH), BF16),
            dma((7 * CHUNKS,)),
            dma((7 * CHUNKS,)),
            dma((CHUNKS * PLANE,)),
            dma((CHUNKS * PLANE,)),
            dma((2 * DEPTH + 2 * PLANE,)),
            dma((2 * DEPTH + 2 * PLANE,)),
            dma((4,)),
            dma((4,)),
            dma((2 + CHUNKS,)),
            dma((2 + CHUNKS,)),
        ],
        compiler_params=pltpu.CompilerParams(
            collective_id=collective_id, has_side_effects=True, vmem_limit_bytes=VMEM_BYTES
        ),
        name=f"back_{c}",
    )(*scalars, *arrays, *picked)


def on_device(
    query_vectors, key_vectors, value_vectors, cotangent, rand_peer, rand_local, global_ids
):
    none = DEPTH * ITEMS
    all_items = jnp.arange(none, dtype=jnp.int32)

    def go(c, collective_id, peers, spots, key, value):
        return fetch(c, global_ids, peers, spots, key, value, collective_id)

    def finish(c, collective_id, query, key, value, grad, fetched):
        got, _, where, plan, halo, shared, *picked = fetched
        count = PLANE * c
        keys = got[:, 0, 2 * LANES : 2 * LANES + c].reshape(count)
        at = jnp.arange(count, dtype=jnp.int32)
        same = keys[None, :] == keys[:, None]
        ahead = at[None, :] < at[:, None]
        before = (keys[None, :] < keys[:, None]) | (same & ahead)
        sorted_at = jnp.sum(before.astype(jnp.int32), axis=1)
        chosen = sorted_at[None, :] == at[:, None]
        order = jnp.sum(jnp.where(chosen, at[None, :], 0), axis=1)
        opens = ~jnp.any(same & ahead, axis=1)
        first = jnp.sum(jnp.where(chosen & opens[None, :], 1, 0), axis=1)
        upto = jnp.sum((keys[None, :] <= all_items[:, None]).astype(jnp.int32), axis=1)
        found = jnp.any(keys[None, :] == all_items[:, None], axis=1)
        ends = jnp.where(found, upto - 1, count)
        return back(
            c,
            (global_ids, where, plan, order, first, ends),
            (query, grad, key, value, halo, shared),
            picked,
            collective_id,
        )

    def usual(query, key, value, grad, peers, spots, *fetched):
        return finish(USUAL, 1, query, key, value, grad, fetched)

    def crowded(query, key, value, grad, peers, spots, *fetched):
        return finish(FULL, 3, query, key, value, grad, go(FULL, 2, peers, spots, key, value))

    fetched = go(USUAL, 0, rand_peer, rand_local, key_vectors, value_vectors)
    return lax.cond(
        fetched[1][0, LANES] > USUAL, crowded, usual,
        query_vectors, key_vectors, value_vectors, cotangent, rand_peer, rand_local, *fetched,
    )


def solution(mesh):
    placed = (
        P("seq", "head"),
        P("seq", "head"),
        P("seq", "head"),
        P("seq", "head"),
        P("head", "seq", None, None),
        P("head", "seq", None, None),
        P(),
    )
    return jax.shard_map(
        on_device,
        mesh=mesh,
        in_specs=placed,
        out_specs=(P(("seq", "head"), None),) * 4,
        check_vma=False,
    )
```

```python
import functools

import jax
import jax.numpy as jnp
from jax import lax
from jax.experimental import pallas as pl
from jax.experimental.pallas import tpu as pltpu
from jax.sharding import PartitionSpec as P

MESH = pl.DeviceIdType.MESH
HEAD_DIM = 128
BLOCK = 64
HEADS_HERE = 8
BLOCKS_HERE = 2
WIDTH = HEADS_HERE * HEAD_DIM
PLANE = 16
DEPTH = 8
ITEMS = BLOCKS_HERE * HEADS_HERE
PICKS = 3 * ITEMS
ROWS = 16
PARTS = BLOCK // ROWS
CHUNKS = 2 * PARTS
LANES = 32
FULL = 2 * DEPTH
FEW = 7
USUAL = 8
SCALE = HEAD_DIM ** (-0.5)
LAST_BLOCK = PLANE * DEPTH * BLOCKS_HERE - 1
VMEM_FULL = 56 * 1024 * 1024
VMEM_USUAL = 44 * 1024 * 1024
F32 = jnp.float32
BF16 = jnp.bfloat16


def position():
    seq = lax.axis_index("seq")
    return seq, lax.div(seq, PLANE), lax.rem(seq, PLANE), lax.axis_index("head")


def signal(seq, head):
    pl.semaphore_signal(
        pltpu.get_barrier_semaphore(), inc=1, device_id=(seq, head), device_id_type=MESH
    )


def remote(src, dst, send, recv, seq, head):
    return pltpu.make_async_remote_copy(
        src_ref=src,
        dst_ref=dst,
        send_sem=send,
        recv_sem=recv,
        device_id=(seq, head),
        device_id_type=MESH,
    )


def ring_hops(q, d):
    return 4 if (d == 0) == (q % 2 == 0) else 3


def ring_slot(q, d, t):
    return sum(ring_hops(q, e) for e in range(d)) + 7 * q + t


def global_block(ids, e):
    return jnp.where(e < HEADS_HERE, ids[0] + ids[1] - LAST_BLOCK, LAST_BLOCK)


def global_place(ids, e):
    block = global_block(ids, e)
    peer = block >> 1
    plane = peer >> 4
    item = plane * ITEMS + (block & 1) * HEADS_HERE + lax.rem(e, HEADS_HERE)
    return plane, peer & (PLANE - 1), item


def write_tables(c, chosen, table, where, plan):
    shape = (PICKS, 128)
    number = lax.broadcasted_iota(jnp.int32, shape, 0)
    lane = lax.broadcasted_iota(jnp.int32, shape, 1)

    parts = []
    for t in range(3):
        for b in range(BLOCKS_HERE):
            parts.append(jnp.broadcast_to(chosen[0, b][:, t : t + 1], (HEADS_HERE, 128)))
    block = jnp.concatenate(parts, axis=0)
    peer, spot = block >> 1, block & 1
    column = peer & (PLANE - 1)
    item = (peer >> 4) * ITEMS + spot * HEADS_HERE + (number & (HEADS_HERE - 1))
    along = jnp.sum(jnp.where(number == lane, column, 0), axis=0, keepdims=True)
    ahead = (column == along) & (lane < number)
    rank = jnp.sum(jnp.where(ahead, 1, 0), axis=1, keepdims=True)
    rank = jnp.broadcast_to(rank, shape)
    most = jnp.max(rank, axis=0, keepdims=True) + 1
    where[...] = jnp.minimum(column * c + rank, PLANE * c - 1)
    group = lane >> 5
    none = DEPTH * ITEMS
    worth = jnp.where(group == 0, item, 0)
    worth = jnp.where(group == 2, item - none, worth)
    worth = jnp.where(group == 3, number, worth)
    here = rank == (lane & (LANES - 1))
    row_group = group[0:1]
    rest = jnp.where(row_group == 2, none, jnp.where(row_group == 1, most, 0))
    for col in range(PLANE):
        line = jnp.sum(jnp.where(here & (column == col), worth, 0), axis=0, keepdims=True)
        line = line + rest
        table[col] = jnp.broadcast_to(line, (8, 128))
        plan[col : col + 1, :] = line


def fetch_kernel(
    c, ids, chosen, key, value, query, grad, got, peak, where, plan, halo, shared, weights, own, sides, both, *rest
):
    terms, rest = rest[:PARTS], rest[PARTS:]
    picked, held, out = rest[0:CHUNKS], rest[CHUNKS : 2 * CHUNKS] + (shared,), rest[2 * CHUNKS : 3 * CHUNKS]
    (
        relay, offer, offered, piece, pieces, slots, spots, table, most, local, local2,
        zsend, zrecv, psend, precv, gsend, grecv, hsend, hrecv, tsend, trecv, msend, mrecv,
    ) = rest[3 * CHUNKS :]
    seq, z, p, head = position()
    place = z * 2 + head

    def table_copy(i):
        peer = lax.rem(p + i, PLANE)
        return remote(
            table.at[peer], got.at[p], tsend.at[i], trecv.at[i], z * PLANE + peer, head
        )

    def most_copy(i):
        other = lax.rem(place + i, 2 * DEPTH)
        return remote(
            most.at[place],
            most.at[place],
            msend.at[i],
            mrecv.at[i],
            lax.div(other, 2) * PLANE + p,
            lax.rem(other, 2),
        )

    def halo_copy(side, kv):
        block = (1 - side) * BLOCK
        other = lax.rem(seq + (1 if side == 0 else PLANE * DEPTH - 1), PLANE * DEPTH)
        return remote(
            (key, value)[kv].at[pl.ds(block, BLOCK)],
            halo.at[side * 2 + kv],
            hsend.at[side * 2 + kv],
            hrecv.at[side * 2 + kv],
            other,
            head,
        )

    def ring_copy(q, d, t):
        step = 1 if d == 0 else DEPTH - 1
        owner = lax.rem(z + t * (DEPTH - step), DEPTH)
        rows = pl.ds(owner * ITEMS, ITEMS)
        slot = ring_slot(q, d, t)
        return remote(
            held[q].at[rows],
            held[q].at[rows],
            zsend.at[slot],
            zrecv.at[slot],
            lax.rem(z + step, DEPTH) * PLANE + p,
            head,
        )

    def plane_copy(q, i):
        peer = lax.rem(p + i, PLANE)
        return remote(
            out[q].at[pl.ds(peer * c, c)],
            picked[q].at[pl.ds(p * c, c)],
            psend.at[q * PLANE + i],
            precv.at[q * PLANE + i],
            z * PLANE + peer,
            head,
        )

    def offer_copy(i):
        peer = lax.rem(p + i, PLANE)
        return remote(
            offer.at[pl.ds(peer * CHUNKS, CHUNKS)],
            offered.at[pl.ds(p * CHUNKS, CHUNKS)],
            gsend.at[i],
            grecv.at[i],
            z * PLANE + peer,
            head,
        )

    def piece_copy(i):
        other = lax.rem(z + i, DEPTH)
        return remote(
            piece.at[other],
            pieces.at[z],
            gsend.at[PLANE + i],
            grecv.at[PLANE + i],
            other * PLANE + p,
            head,
        )

    def relay_copy(i):
        return remote(
            relay,
            shared.at[z * PLANE + p],
            gsend.at[PLANE + DEPTH + i],
            grecv.at[PLANE + DEPTH + i],
            z * PLANE + lax.rem(p + i, PLANE),
            head,
        )

    def offers(sender, peer):
        return (peer < HEADS_HERE) | (sender == PLANE - 1)

    def offer_start():
        for e in range(PLANE):
            second = (global_block(ids, e) & 1) == 1
            j = e % HEADS_HERE
            for q in range(CHUNKS):
                low, high = [
                    (key, value)[q // PARTS][
                        b * BLOCK + (q % PARTS) * ROWS : b * BLOCK + (q % PARTS + 1) * ROWS,
                        j * HEAD_DIM : (j + 1) * HEAD_DIM,
                    ]
                    for b in range(BLOCKS_HERE)
                ]
                offer[e * CHUNKS + q] = jnp.where(second, high, low)

        @pl.loop(1, PLANE)
        def _(i):
            @pl.when(offers(p, lax.rem(p + i, PLANE)))
            def _():
                offer_copy(i).start()

        mine = pl.ds(p * CHUNKS, CHUNKS)
        offered[mine] = offer[mine]

    def piece_start():
        @pl.loop(1, PLANE)
        def _(i):
            @pl.when(offers(lax.rem(p + PLANE - i, PLANE), p))
            def _():
                offer_copy(i).wait_recv()

        _, column, _ = global_place(ids, p)
        for q in range(CHUNKS):
            found = offered[(PLANE - 1) * CHUNKS + q]
            for source in range(PLANE - 1):
                found = jnp.where(column == source, offered[source * CHUNKS + q], found)
            piece[q] = found

        @pl.loop(1, DEPTH)
        def _(i):
            piece_copy(i).start()

        pieces[z] = piece[z]

    def relay_start():
        @pl.loop(1, DEPTH)
        def _(i):
            piece_copy(i).wait_recv()

        plane, _, _ = global_place(ids, p)
        found = pieces[DEPTH - 1]
        for source in range(DEPTH - 1):
            found = jnp.where(plane == source, pieces[source], found)
        relay[...] = found
        shared[z * PLANE + p] = relay[...]

        @pl.loop(1, PLANE)
        def _(i):
            relay_copy(i).start()

    def relay_wait():
        @pl.loop(1, PLANE)
        def _(i):
            relay_copy(i).wait_recv()

    def fill(q):
        source, part = (key, value)[q // PARTS], q % PARTS
        for b in range(BLOCKS_HERE):
            for j in range(HEADS_HERE):
                held[q][z * ITEMS + b * HEADS_HERE + j] = source[
                    b * BLOCK + part * ROWS : b * BLOCK + (part + 1) * ROWS,
                    j * HEAD_DIM : (j + 1) * HEAD_DIM,
                ]

    def ring_start(q):
        for d in range(2):
            ring_copy(q, d, 0).start()

    def ring_step(q, t):
        for d in range(2):
            if t < ring_hops(q, d):
                ring_copy(q, d, t).wait_recv()
                if t + 1 < ring_hops(q, d):
                    ring_copy(q, d, t + 1).start()

    def spread(q):
        @pl.loop(1, PLANE)
        def _(i):
            peer = lax.rem(p + i, PLANE)
            for s in range(c):
                out[q][peer * c + s] = held[q][slots[peer, 0, s]]
            plane_copy(q, i).start()

        for s in range(c):
            picked[q][p * c + s] = held[q][slots[p, 0, s]]

    fill(0)

    @pl.loop(1, 2 * DEPTH)
    def _(i):
        other = lax.rem(place + i, 2 * DEPTH)
        signal(lax.div(other, 2) * PLANE + p, lax.rem(other, 2))

    @pl.loop(1, PLANE)
    def _(i):
        signal(z * PLANE + lax.rem(p + i, PLANE), head)

    for step in (1, PLANE * DEPTH - 1):
        signal(lax.rem(seq + step, PLANE * DEPTH), head)
    pl.semaphore_wait(pltpu.get_barrier_semaphore(), 2 * DEPTH - 1 + PLANE - 1 + 2)

    ring_start(0)
    fill(1)
    ring_start(1)
    write_tables(c, chosen, table, where, plan)
    spot_copy = pltpu.make_async_copy(where, spots, local2)
    spot_copy.start()

    @pl.loop(1, PLANE)
    def _(i):
        table_copy(i).start()

    got[p] = table[p]
    offer_start()
    for q in range(2, CHUNKS):
        fill(q)
    for side in range(2):
        for kv in range(2):
            halo_copy(side, kv).start()

    for step in range(CHUNKS + 4):
        for t in range(3, -1, -1):
            if 0 <= step - t <= CHUNKS:
                ring_step(step - t, t)
        if step + 2 == CHUNKS:
            relay_wait()
        if step + 2 <= CHUNKS:
            ring_start(step + 2)
        if step == 1:
            piece_start()
        if step == 3:
            relay_start()
        if step == 2:

            @pl.loop(1, PLANE)
            def _(i):
                table_copy(i).wait()

            to_scalars = pltpu.make_async_copy(got, slots, local)
            to_scalars.start()
            to_scalars.wait()
        if 0 <= step - 3 < CHUNKS:
            spread(step - 3)
        if step == 4:
            most[place] = jnp.max(got[...], axis=0)

            @pl.loop(1, 2 * DEPTH)
            def _(i):
                most_copy(i).start()

    spot_copy.wait()
    for side in range(2):
        for kv in range(2):
            halo_copy(side, kv).wait()
    for q in range(PARTS):

        @pl.loop(1, PLANE)
        def _(i):
            plane_copy(q, i).wait_recv()

    @pl.loop(0, HEADS_HERE)
    def _(j):
        cols = columns_of(j)
        keys, far_keys = listed(spots, picked, halo, shared, key, 0, j)
        w_near, w_far = softmax(seq, keys, far_keys, query[:, cols])
        weights[j, : 6 * BLOCK] = w_near
        weights[j, 6 * BLOCK :] = w_far
        scatter(j, w_near.astype(BF16), w_far.astype(BF16), grad[:, cols], own, sides, both, terms)

    @pl.loop(1, 2 * DEPTH)
    def _(i):
        most_copy(i).wait()

    peak[...] = jnp.max(most[...], axis=0)
    @pl.loop(1, PLANE)
    def _(i):
        @pl.when(offers(p, lax.rem(p + i, PLANE)))
        def _():
            offer_copy(i).wait_send()

        relay_copy(i).wait_send()

    @pl.loop(1, DEPTH)
    def _(i):
        piece_copy(i).wait_send()

    for q in range(CHUNKS + 1):
        if q < CHUNKS:

            @pl.loop(1, PLANE)
            def _(i):
                if q >= PARTS:
                    plane_copy(q, i).wait_recv()
                plane_copy(q, i).wait_send()

        for d in range(2):
            for t in range(ring_hops(q, d)):
                ring_copy(q, d, t).wait_send()


def fetch(c, ids, chosen, key, value, query, grad, collective_id):
    smem = pl.BlockSpec(memory_space=pltpu.SMEM)
    vmem = pl.BlockSpec(memory_space=pltpu.VMEM)
    part = jax.ShapeDtypeStruct((PLANE * c, ROWS, HEAD_DIM), BF16)
    rows = jax.ShapeDtypeStruct((PLANE, 8, 128), jnp.int32)
    dma = pltpu.SemaphoreType.DMA
    return pl.pallas_call(
        functools.partial(fetch_kernel, c),
        out_shape=(
            rows,
            jax.ShapeDtypeStruct((8, 128), jnp.int32),
            jax.ShapeDtypeStruct((PICKS, 128), jnp.int32),
            jax.ShapeDtypeStruct((PLANE, 128), jnp.int32),
            jax.ShapeDtypeStruct((4, BLOCK, WIDTH), BF16),
            jax.ShapeDtypeStruct((CHUNKS * PLANE, ROWS, HEAD_DIM), BF16),
            jax.ShapeDtypeStruct((HEADS_HERE, 9 * BLOCK, 128), F32),
            jax.ShapeDtypeStruct((PARTS * ITEMS, ROWS, HEAD_DIM), F32),
            jax.ShapeDtypeStruct((2 * PARTS * HEADS_HERE, ROWS, HEAD_DIM), BF16),
            jax.ShapeDtypeStruct((PLANE * PARTS, ROWS, HEAD_DIM), BF16),
        )
        + (jax.ShapeDtypeStruct((PICKS, ROWS, HEAD_DIM), BF16),) * PARTS
        + (part,) * CHUNKS,
        in_specs=[smem] + [vmem] * 5,
        out_specs=(vmem,) * (10 + PARTS + CHUNKS),
        scratch_shapes=[pltpu.VMEM((DEPTH * ITEMS, ROWS, HEAD_DIM), BF16)] * CHUNKS
        + [pltpu.VMEM(part.shape, BF16)] * CHUNKS
        + [
            pltpu.VMEM((ROWS, HEAD_DIM), BF16),
            pltpu.VMEM((PLANE * CHUNKS, ROWS, HEAD_DIM), BF16),
            pltpu.VMEM((PLANE * CHUNKS, ROWS, HEAD_DIM), BF16),
            pltpu.VMEM((DEPTH, ROWS, HEAD_DIM), BF16),
            pltpu.VMEM((DEPTH, ROWS, HEAD_DIM), BF16),
            pltpu.SMEM((PLANE, 8, 128), jnp.int32),
            pltpu.SMEM((PICKS, 128), jnp.int32),
            pltpu.VMEM((PLANE, 8, 128), jnp.int32),
            pltpu.VMEM((2 * DEPTH, 8, 128), jnp.int32),
            dma(()),
            dma(()),
            dma((7 * (CHUNKS + 1),)),
            dma((7 * (CHUNKS + 1),)),
            dma((CHUNKS * PLANE,)),
            dma((CHUNKS * PLANE,)),
            dma((2 * PLANE + DEPTH,)),
            dma((2 * PLANE + DEPTH,)),
            dma((4,)),
            dma((4,)),
            dma((PLANE,)),
            dma((PLANE,)),
            dma((2 * DEPTH,)),
            dma((2 * DEPTH,)),
        ],
        compiler_params=pltpu.CompilerParams(
            collective_id=collective_id, has_side_effects=True, vmem_limit_bytes=VMEM_FULL if c == FULL else VMEM_USUAL
        ),
        name=f"fetch_{c}",
    )(ids, chosen, key, value, query, grad)


def dot(a, b, contract):
    return lax.dot_general(a, b, ((contract[0:1], contract[1:2]), ((), ())), preferred_element_type=F32)


def columns_of(j):
    return pl.ds(pl.multiple_of(j * HEAD_DIM, HEAD_DIM), HEAD_DIM)


def listed(where, picked, halo, shared, rows, kv, j):
    cols = columns_of(j)
    close = [halo[kv, :, cols], rows[:, cols], halo[2 + kv, :, cols]]
    for group in range(2):
        for part in range(PARTS):
            close.append(shared[(kv * PARTS + part) * PLANE + group * HEADS_HERE + j])
    far = []
    for b in range(BLOCKS_HERE):
        pieces = []
        for t in range(3):
            at = where[t * ITEMS + b * HEADS_HERE + j, 0]
            for part in range(PARTS):
                pieces.append(picked[kv * PARTS + part][at])
        far.append(jnp.concatenate(pieces, axis=0))
    return jnp.concatenate(close, axis=0), far


def first_block():
    return lax.broadcasted_iota(jnp.int32, (3 * BLOCK, 128), 1) < BLOCK


def products(close, far, other):
    a = dot(close, other, (1, 1))
    b = jnp.where(first_block(), dot(far[0], other, (1, 1)), dot(far[1], other, (1, 1)))
    return a, b


def gather(near_w, far_w, close, far):
    total = dot(near_w, close, (0, 0))
    top_rows = dot(far_w, far[0], (0, 0))
    low_rows = dot(far_w, far[1], (0, 0))
    return total + jnp.concatenate([top_rows[:BLOCK], low_rows[BLOCK:]], axis=0)


def scatter(j, weight_near, weight_far, rows_here, own, sides, both, terms):
    near_terms = dot(weight_near, rows_here, (1, 0))
    zero = jnp.zeros_like(weight_far)
    far_terms = (
        dot(jnp.where(first_block(), weight_far, zero), rows_here, (1, 0)).astype(BF16),
        dot(jnp.where(first_block(), zero, weight_far), rows_here, (1, 0)).astype(BF16),
    )
    for part in range(PARTS):

        def piece(block):
            start = block * BLOCK + part * ROWS
            return near_terms[start : start + ROWS]

        sides[part * HEADS_HERE + j] = piece(0).astype(BF16)
        sides[(PARTS + part) * HEADS_HERE + j] = piece(3).astype(BF16)
        for b in range(BLOCKS_HERE):
            own[part * ITEMS + b * HEADS_HERE + j] = piece(1 + b)
            for t in range(3):
                start = t * BLOCK + part * ROWS
                terms[part][t * ITEMS + b * HEADS_HERE + j] = far_terms[b][start : start + ROWS]
        for group in range(2):
            both[(group * HEADS_HERE + j) * PARTS + part] = piece(4 + group).astype(BF16)


def softmax(seq, keys, far_keys, queries):
    near = 4 * BLOCK
    rows = lax.broadcasted_iota(jnp.int32, (near, 128), 0)
    lanes = lax.broadcasted_iota(jnp.int32, (near, 128), 1)
    hidden = (
        ((lanes < BLOCK) & (rows >= 3 * BLOCK))
        | ((lanes >= BLOCK) & (rows < BLOCK))
        | ((rows < BLOCK) & (seq == 0))
        | ((rows >= 3 * BLOCK) & (seq == PLANE * DEPTH - 1))
    )
    s_near, s_far = products(keys, far_keys, queries)
    s_near = s_near * SCALE
    s_far = s_far * SCALE
    s_near = jnp.concatenate([jnp.where(hidden, -1e30, s_near[:near]), s_near[near:]], axis=0)
    top = jnp.maximum(
        jnp.max(s_near, axis=0, keepdims=True), jnp.max(s_far, axis=0, keepdims=True)
    )
    w_near = jnp.exp(s_near - top)
    w_far = jnp.exp(s_far - top)
    total = jnp.sum(w_near, axis=0, keepdims=True) + jnp.sum(w_far, axis=0, keepdims=True)
    inverse = 1.0 / total
    return w_near * inverse, w_far * inverse


def back_kernel(
    c, ids, where, plan, order, first, ends, query, grad, key, value, halo, shared, weights, own_v, sides_v, both_v, *rest
):
    terms_v, rest = rest[:PARTS], rest[PARTS:]
    picked, rest = rest[:CHUNKS], rest[CHUNKS:]
    outs, rest = rest[:4], rest[4:]
    terms_k, rest = rest[:PARTS], rest[PARTS:]
    out, rest = rest[:CHUNKS], rest[CHUNKS:]
    arrived, rest = rest[:CHUNKS], rest[CHUNKS:]
    totals, rest = rest[:CHUNKS], rest[CHUNKS:]
    (
        attended, grad_query, own_k, sides_k, both_k,
        zone_in, zone, tile_in, extras, relay, runs, zout, zin, beside, cross,
        zsend, zrecv, psend, precv, gsend, grecv, hsend, hrecv, csend, crecv,
    ) = rest
    seq, z, p, head = position()

    @pl.loop(1, PLANE)
    def _(i):
        signal(z * PLANE + lax.rem(p + i, PLANE), head)

    @pl.loop(1, DEPTH)
    def _(i):
        signal(lax.rem(z + i, DEPTH) * PLANE + p, head)

    for step in (1, PLANE * DEPTH - 1):
        signal(lax.rem(seq + step, PLANE * DEPTH), head)
    signal(seq, 1 - head)

    terms = terms_k + terms_v
    own, sides, both = (own_k, own_v), (sides_k, sides_v), (both_k, both_v)

    def backward(j):
        cols = columns_of(j)
        q, g = query[:, cols], grad[:, cols]
        keys, far_keys = listed(where, picked, halo, shared, key, 0, j)
        values, far_values = listed(where, picked, halo, shared, value, 1, j)
        w_near, w_far = weights[j, : 6 * BLOCK], weights[j, 6 * BLOCK :]
        gw_near, gw_far = products(values, far_values, g)
        centre = jnp.sum(w_near * gw_near, axis=0, keepdims=True) + jnp.sum(
            w_far * gw_far, axis=0, keepdims=True
        )
        d_near = (w_near * (gw_near - centre) * SCALE).astype(BF16)
        d_far = (w_far * (gw_far - centre) * SCALE).astype(BF16)
        scatter(j, d_near, d_far, q, own_k, sides_k, both_k, terms_k)
        attended[:, cols] = gather(
            w_near.astype(BF16), w_far.astype(BF16), values, far_values
        ).astype(BF16)
        grad_query[:, cols] = gather(d_near, d_far, keys, far_keys).astype(BF16)

    count = PLANE * c
    mine = pl.ds(pl.multiple_of(head * WIDTH, WIDTH), WIDTH)

    def result_copy(k):
        source = (attended, grad_query)[k].at[pl.ds((1 - head) * BLOCK, BLOCK)]
        return remote(source, outs[k].at[:, mine], csend.at[k], crecv.at[k], seq, 1 - head)

    def cross_copy(q):
        return remote(
            cross.at[q],
            outs[2 + q // PARTS].at[pl.ds((q % PARTS) * ROWS, ROWS), mine],
            csend.at[2 + q],
            crecv.at[2 + q],
            seq,
            1 - head,
        )

    def side_copy(kv, side):
        size = PARTS * HEADS_HERE
        other = lax.rem(seq + (PLANE * DEPTH - 1 if side == 0 else 1), PLANE * DEPTH)
        return remote(
            sides[kv].at[pl.ds(side * size, size)],
            beside.at[pl.ds(((1 - side) * 2 + kv) * size, size)],
            hsend.at[kv * 2 + side],
            hrecv.at[kv * 2 + side],
            other,
            head,
        )

    def plane_copy(q, i):
        peer = lax.rem(p + i, PLANE)
        return remote(
            out[q].at[pl.ds(peer * c, c)],
            arrived[q].at[pl.ds(p * c, c)],
            psend.at[q * PLANE + i],
            precv.at[q * PLANE + i],
            z * PLANE + peer,
            head,
        )

    def zone_copy(kv, i):
        other = lax.rem(z + i, DEPTH)
        rows = pl.ds(other * 2 * PARTS, 2 * PARTS)
        return remote(
            both[kv].at[rows],
            zone_in.at[pl.ds((kv * DEPTH + z) * 2 * PARTS, 2 * PARTS)],
            gsend.at[kv * DEPTH + i],
            grecv.at[kv * DEPTH + i],
            other * PLANE + p,
            head,
        )

    def tile_copy(kv, i):
        peer = lax.rem(p + i, PLANE)
        return remote(
            zone.at[kv * 2 * PARTS + lax.rem(peer, 2 * PARTS)],
            tile_in.at[p],
            gsend.at[2 * DEPTH + i],
            grecv.at[2 * DEPTH + i],
            z * PLANE + peer,
            head,
        )

    def total_copy(i):
        peer = lax.rem(p + i, PLANE)
        return remote(
            relay,
            extras.at[z * PLANE + p],
            gsend.at[2 * DEPTH + PLANE + i],
            grecv.at[2 * DEPTH + PLANE + i],
            z * PLANE + peer,
            head,
        )

    def adds(kv, q):
        return lax.div(q, 2 * PARTS) == 1 - kv

    def zone_start(kv):
        @pl.loop(1, DEPTH)
        def _(i):
            zone_copy(kv, i).start()

    def zone_add(kv):
        @pl.loop(1, DEPTH)
        def _(i):
            zone_copy(kv, i).wait_recv()

        size = 2 * PARTS
        total = both[kv][pl.ds(z * size, size)].astype(F32)
        for i in range(1, DEPTH):
            other = lax.rem(z + i, DEPTH)
            total = total + zone_in[pl.ds((kv * DEPTH + other) * size, size)].astype(F32)
        zone[kv * size : (kv + 1) * size] = total.astype(BF16)

        @pl.loop(1, PLANE)
        def _(i):
            @pl.when(adds(kv, lax.rem(p + i, PLANE)))
            def _():
                tile_copy(kv, i).start()

    def tile_add(kv):
        @pl.when(adds(kv, p))
        def _():
            @pl.loop(1, PLANE)
            def _(i):
                tile_copy(kv, i).wait_recv()

            tile_in[p] = zone[kv * 2 * PARTS + lax.rem(p, 2 * PARTS)]
            total = tile_in[0].astype(F32)
            for i in range(1, PLANE):
                total = total + tile_in[i].astype(F32)
            relay[...] = total.astype(BF16)
            extras[z * PLANE + p] = relay[...]

            @pl.loop(1, PLANE)
            def _(i):
                total_copy(i).start()

    def extra_copy(kv, d, t):
        step = 1 if d == 0 else DEPTH - 1
        owner = lax.rem(z + t * (DEPTH - step), DEPTH)
        rows = pl.ds(owner * PLANE + (1 - kv) * 2 * PARTS, 2 * PARTS)
        slot = ring_slot(CHUNKS + kv, d, t)
        return remote(
            extras.at[rows],
            extras.at[rows],
            zsend.at[slot],
            zrecv.at[slot],
            lax.rem(z + step, DEPTH) * PLANE + p,
            head,
        )

    def extra_step(kv, t):
        for d in range(2):
            hops = ring_hops(CHUNKS + kv, d)
            if 0 < t <= hops:
                extra_copy(kv, d, t - 1).wait_recv()
            if t < hops:
                extra_copy(kv, d, t).start()

    def total_wait(kv):
        @pl.loop(1, PLANE)
        def _(i):
            @pl.when(adds(kv, lax.rem(p + PLANE - i, PLANE)))
            def _():
                total_copy(i).wait_recv()

    def ring_copy(q, d, t):
        step = 1 if d == 0 else DEPTH - 1
        slot = ring_slot(q, d, t)
        return remote(
            zout.at[slot],
            zin.at[slot],
            zsend.at[slot],
            zrecv.at[slot],
            lax.rem(z + step, DEPTH) * PLANE + p,
            head,
        )

    def spread(q):
        @pl.loop(1, PLANE)
        def _(i):
            peer = lax.rem(p + i, PLANE)
            for s in range(c):
                out[q][peer * c + s] = terms[q][plan[peer, 3 * LANES + s]]
            plane_copy(q, i).start()

        for s in range(c):
            arrived[q][p * c + s] = terms[q][plan[p, 3 * LANES + s]]

    def collect(q):
        @pl.loop(1, PLANE)
        def _(i):
            plane_copy(q, i).wait_recv()

        def add(r, total):
            term = arrived[q][order[r]].astype(F32)
            total = jnp.where(first[r] == 1, term, total + term)
            runs[r] = total
            return total

        lax.fori_loop(0, count, add, jnp.zeros((ROWS, HEAD_DIM), F32), unroll=8)

        @pl.loop(0, DEPTH * ITEMS, unroll=8)
        def _(i):
            totals[q][i] = runs[ends[i]]

    def ring_step(q, t):
        for d in range(2):
            hops = ring_hops(q, d)
            if t < hops:
                away = hops - t
                target = lax.rem(z + (away if d == 0 else DEPTH - away), DEPTH)
                partial = totals[q][pl.ds(target * ITEMS, ITEMS)]
                if t > 0:
                    ring_copy(q, d, t - 1).wait_recv()
                    partial = partial + zin[ring_slot(q, d, t - 1)].astype(F32)
                zout[ring_slot(q, d, t)] = partial.astype(BF16)
                ring_copy(q, d, t).start()

    def finish(q):
        for d in range(2):
            ring_copy(q, d, ring_hops(q, d) - 1).wait_recv()
        kv, part = q // PARTS, q % PARTS
        for j in range(HEADS_HERE):
            for stays in range(2):
                b = head if stays else 1 - head
                item = b * HEADS_HERE + j
                total = totals[q][z * ITEMS + item] + own[kv][part * ITEMS + item]
                total = total + beside[(b * CHUNKS + q) * HEADS_HERE + j].astype(F32)
                for d in range(2):
                    total = total + zin[ring_slot(q, d, ring_hops(q, d) - 1), item].astype(F32)
                for group in range(2):
                    e = group * HEADS_HERE + j
                    tile = (e // 2) * PLANE + (1 - kv) * 2 * PARTS + (e % 2) * PARTS + part
                    mine_too = global_block(ids, e) == seq * BLOCKS_HERE + b
                    total = total + jnp.where(mine_too, extras[tile].astype(F32), 0.0)
                total = total.astype(BF16)
                if stays:
                    cols = pl.ds(pl.multiple_of(head * WIDTH + j * HEAD_DIM, HEAD_DIM), HEAD_DIM)
                    outs[2 + kv][part * ROWS : (part + 1) * ROWS, cols] = total
                else:
                    cross[q, :, j * HEAD_DIM : (j + 1) * HEAD_DIM] = total
        cross_copy(q).start()

    runs[count] = jnp.zeros((ROWS, HEAD_DIM), F32)
    pl.semaphore_wait(pltpu.get_barrier_semaphore(), PLANE + DEPTH + 1)
    turn = list(range(PARTS, CHUNKS)) + list(range(PARTS))
    zone_start(1)
    spread(turn[0])

    @pl.loop(0, HEADS_HERE)
    def _(j):
        backward(j)

    zone_start(0)
    spread(turn[1])
    zone_add(1)
    spread(turn[2])
    for k in range(2):
        result_copy(k).start()
        outs[k][:, mine] = (attended, grad_query)[k][pl.ds(pl.multiple_of(head * BLOCK, BLOCK), BLOCK)]
    for step in range(CHUNKS + 5):
        if 0 < step and step + 2 < CHUNKS:
            spread(turn[step + 2])
        if step == CHUNKS - 3:
            for kv in (1, 0):
                for side in range(2):
                    side_copy(kv, side).start()
        if step == 1:
            tile_add(1)
            zone_add(0)
        if step == 3:
            tile_add(0)
            total_wait(1)
        if step == 5:
            total_wait(0)
        for kv in range(2):
            if 0 <= step - (5 - 2 * kv) <= 4:
                extra_step(kv, step - (5 - 2 * kv))
        for t in range(3, 0, -1):
            if 0 <= step - t < CHUNKS:
                ring_step(turn[step - t], t)
        if step < CHUNKS:
            collect(turn[step])
            ring_step(turn[step], 0)
        for n, q in enumerate(turn):
            if step == (9, 9, 9, 10, 10, 10, 11, 11)[n]:
                if n % PARTS == 0:
                    for side in range(2):
                        side_copy(q // PARTS, side).wait()
                finish(q)
    for kv in range(2):

        @pl.loop(1, DEPTH)
        def _(i):
            zone_copy(kv, i).wait_send()

        @pl.loop(1, PLANE)
        def _(i):
            @pl.when(adds(kv, lax.rem(p + i, PLANE)))
            def _():
                tile_copy(kv, i).wait_send()

    @pl.loop(1, PLANE)
    def _(i):
        total_copy(i).wait_send()

    for kv in range(2):
        for d in range(2):
            for t in range(ring_hops(CHUNKS + kv, d)):
                extra_copy(kv, d, t).wait_send()
    for q in range(CHUNKS):

        @pl.loop(1, PLANE)
        def _(i):
            plane_copy(q, i).wait_send()

        for d in range(2):
            for t in range(ring_hops(q, d)):
                ring_copy(q, d, t).wait_send()
        cross_copy(q).wait()
    for k in range(2):
        result_copy(k).wait()


def back(c, scalars, arrays, tiles, collective_id):
    smem = pl.BlockSpec(memory_space=pltpu.SMEM)
    vmem = pl.BlockSpec(memory_space=pltpu.VMEM)
    dma = pltpu.SemaphoreType.DMA
    vm = pltpu.VMEM
    tile = (ROWS, HEAD_DIM)
    part = (PLANE * c,) + tile
    return pl.pallas_call(
        functools.partial(back_kernel, c),
        out_shape=(jax.ShapeDtypeStruct((BLOCK, 2 * WIDTH), BF16),) * 4,
        in_specs=[smem] * len(scalars) + [vmem] * (len(arrays) + len(tiles)),
        out_specs=(vmem,) * 4,
        scratch_shapes=[vm((PICKS,) + tile, BF16)] * PARTS
        + [vm(part, BF16)] * (2 * CHUNKS)
        + [vm((DEPTH * ITEMS,) + tile, F32)] * CHUNKS
        + [
            vm((BLOCKS_HERE * BLOCK, WIDTH), BF16),
            vm((BLOCKS_HERE * BLOCK, WIDTH), BF16),
            vm((PARTS * ITEMS,) + tile, F32),
            vm((2 * PARTS * HEADS_HERE,) + tile, BF16),
            vm((PLANE * PARTS,) + tile, BF16),
            vm((2 * DEPTH * 2 * PARTS,) + tile, BF16),
            vm((2 * 2 * PARTS,) + tile, BF16),
            vm((PLANE,) + tile, BF16),
            vm((DEPTH * PLANE,) + tile, BF16),
            vm(tile, BF16),
            vm((PLANE * c + 1,) + tile, F32),
            vm((7 * CHUNKS, ITEMS) + tile, BF16),
            vm((7 * CHUNKS, ITEMS) + tile, BF16),
            vm((2 * CHUNKS * HEADS_HERE,) + tile, BF16),
            vm((CHUNKS, ROWS, WIDTH), BF16),
            dma((7 * (CHUNKS + 2),)),
            dma((7 * (CHUNKS + 2),)),
            dma((CHUNKS * PLANE,)),
            dma((CHUNKS * PLANE,)),
            dma((2 * DEPTH + 2 * PLANE,)),
            dma((2 * DEPTH + 2 * PLANE,)),
            dma((4,)),
            dma((4,)),
            dma((2 + CHUNKS,)),
            dma((2 + CHUNKS,)),
        ],
        compiler_params=pltpu.CompilerParams(
            collective_id=collective_id, has_side_effects=True, vmem_limit_bytes=VMEM_FULL if c == FULL else VMEM_USUAL
        ),
        name=f"back_{c}",
    )(*scalars, *arrays, *tiles)


def on_device(
    query_vectors, key_vectors, value_vectors, cotangent, rand_peer, rand_local, global_ids
):
    none = DEPTH * ITEMS
    all_items = jnp.arange(none, dtype=jnp.int32)

    def go(c, collective_id, query, key, value, grad, chosen):
        return fetch(c, global_ids, chosen, key, value, query, grad, collective_id)

    def finish(c, collective_id, query, key, value, grad, fetched):
        got, _, where, plan, halo, shared, weights, own, sides, both, *tiles = fetched
        count = PLANE * c
        keys = got[:, 0, 2 * LANES : 2 * LANES + c].reshape(count)
        at = jnp.arange(count, dtype=jnp.int32)
        same = keys[None, :] == keys[:, None]
        ahead = at[None, :] < at[:, None]
        before = (keys[None, :] < keys[:, None]) | (same & ahead)
        sorted_at = jnp.sum(before.astype(jnp.int32), axis=1)
        chosen = sorted_at[None, :] == at[:, None]
        order = jnp.sum(jnp.where(chosen, at[None, :], 0), axis=1)
        opens = ~jnp.any(same & ahead, axis=1)
        first = jnp.sum(jnp.where(chosen & opens[None, :], 1, 0), axis=1)
        upto = jnp.sum((keys[None, :] <= all_items[:, None]).astype(jnp.int32), axis=1)
        found = jnp.any(keys[None, :] == all_items[:, None], axis=1)
        ends = jnp.where(found, upto - 1, count)
        return back(
            c,
            (global_ids, where, plan, order, first, ends),
            (query, grad, key, value, halo, shared, weights, own, sides, both),
            tiles,
            collective_id,
        )

    def few(*args):
        return finish(FEW, 4, *args[:4], args[5:])

    def usual(*args):
        return finish(USUAL, 1, *args[:4], args[5:])

    def crowded(*args):
        return finish(FULL, 3, *args[:4], go(FULL, 2, *args[:5]))

    args = (query_vectors, key_vectors, value_vectors, cotangent, rand_peer * BLOCKS_HERE + rand_local)
    fetched = go(USUAL, 0, *args)
    peak = fetched[1][0, LANES]
    level = (peak > FEW).astype(jnp.int32) + (peak > USUAL).astype(jnp.int32)
    return lax.switch(level, (few, usual, crowded), *args, *fetched)


def solution(mesh):
    placed = (
        P("seq", "head"),
        P("seq", "head"),
        P("seq", "head"),
        P("seq", "head"),
        P("head", "seq", None, None),
        P("head", "seq", None, None),
        P(),
    )
    return jax.shard_map(
        on_device,
        mesh=mesh,
        in_specs=placed,
        out_specs=(P(("seq", "head"), None),) * 4,
        check_vma=False,
    )
```

```python
import functools

import jax
import jax.numpy as jnp
from jax import lax
from jax.experimental import pallas as pl
from jax.experimental.pallas import tpu as pltpu
from jax.sharding import PartitionSpec as P

MESH = pl.DeviceIdType.MESH
HEAD_DIM = 128
BLOCK = 64
HEADS_HERE = 8
BLOCKS_HERE = 2
WIDTH = HEADS_HERE * HEAD_DIM
PLANE = 16
DEPTH = 8
ITEMS = BLOCKS_HERE * HEADS_HERE
PICKS = 3 * ITEMS
ROWS = 16
PARTS = BLOCK // ROWS
CHUNKS = 2 * PARTS
LANES = 32
FULL = 2 * DEPTH
USUAL = 8
LAST_BLOCK = PLANE * DEPTH * BLOCKS_HERE - 1
VMEM_BYTES = 56 * 1024 * 1024
F32 = jnp.float32
BF16 = jnp.bfloat16


def position():
    seq = lax.axis_index("seq")
    return seq, lax.div(seq, PLANE), lax.rem(seq, PLANE), lax.axis_index("head")


def signal(seq, head):
    pl.semaphore_signal(
        pltpu.get_barrier_semaphore(), inc=1, device_id=(seq, head), device_id_type=MESH
    )


def remote(src, dst, send, recv, seq, head):
    return pltpu.make_async_remote_copy(
        src_ref=src,
        dst_ref=dst,
        send_sem=send,
        recv_sem=recv,
        device_id=(seq, head),
        device_id_type=MESH,
    )


def ring_hops(q, d):
    return 4 if (d == 0) == (q % 2 == 0) else 3


def ring_slot(q, d, t):
    return sum(ring_hops(q, e) for e in range(d)) + 7 * q + t


def global_block(ids, e):
    return jnp.where(e < HEADS_HERE, ids[0] + ids[1] - LAST_BLOCK, LAST_BLOCK)


def global_place(ids, e):
    block = global_block(ids, e)
    peer = block >> 1
    plane = peer >> 4
    item = plane * ITEMS + (block & 1) * HEADS_HERE + lax.rem(e, HEADS_HERE)
    return plane, peer & (PLANE - 1), item


def write_tables(c, rand_peer, rand_local, table, where, plan):
    shape = (PICKS, 128)
    number = lax.broadcasted_iota(jnp.int32, shape, 0)
    lane = lax.broadcasted_iota(jnp.int32, shape, 1)

    def spread_out(ref):
        parts = []
        for t in range(3):
            for b in range(BLOCKS_HERE):
                parts.append(jnp.broadcast_to(ref[0, b][:, t : t + 1], (HEADS_HERE, 128)))
        return jnp.concatenate(parts, axis=0)

    peer, spot = spread_out(rand_peer), spread_out(rand_local)
    column = peer & (PLANE - 1)
    item = (peer >> 4) * ITEMS + spot * HEADS_HERE + (number & (HEADS_HERE - 1))
    along = jnp.sum(jnp.where(number == lane, column, 0), axis=0, keepdims=True)
    ahead = (column == along) & (lane < number)
    rank = jnp.sum(jnp.where(ahead, 1, 0), axis=1, keepdims=True)
    rank = jnp.broadcast_to(rank, shape)
    most = jnp.max(rank, axis=0, keepdims=True) + 1
    where[...] = jnp.minimum(column * c + rank, PLANE * c - 1)
    group = lane >> 5
    none = DEPTH * ITEMS
    worth = jnp.where(group == 0, item, 0)
    worth = jnp.where(group == 2, item - none, worth)
    worth = jnp.where(group == 3, number, worth)
    here = rank == (lane & (LANES - 1))
    row_group = group[0:1]
    rest = jnp.where(row_group == 2, none, jnp.where(row_group == 1, most, 0))
    for col in range(PLANE):
        line = jnp.sum(jnp.where(here & (column == col), worth, 0), axis=0, keepdims=True)
        line = line + rest
        table[col] = jnp.broadcast_to(line, (8, 128))
        plan[col : col + 1, :] = line


def fetch_kernel(c, ids, rand_peer, rand_local, key, value, got, peak, where, plan, halo, shared, *rest):
    picked, held, out = rest[0:CHUNKS], rest[CHUNKS : 2 * CHUNKS] + (shared,), rest[2 * CHUNKS : 3 * CHUNKS]
    (
        relay, offer, offered, piece, pieces, slots, table, most, local,
        zsend, zrecv, psend, precv, gsend, grecv, hsend, hrecv, tsend, trecv, msend, mrecv,
    ) = rest[3 * CHUNKS :]
    seq, z, p, head = position()
    place = z * 2 + head

    def table_copy(i):
        peer = lax.rem(p + i, PLANE)
        return remote(
            table.at[peer], got.at[p], tsend.at[i], trecv.at[i], z * PLANE + peer, head
        )

    def most_copy(i):
        other = lax.rem(place + i, 2 * DEPTH)
        return remote(
            most.at[place],
            most.at[place],
            msend.at[i],
            mrecv.at[i],
            lax.div(other, 2) * PLANE + p,
            lax.rem(other, 2),
        )

    def halo_copy(side, kv):
        block = (1 - side) * BLOCK
        other = lax.rem(seq + (1 if side == 0 else PLANE * DEPTH - 1), PLANE * DEPTH)
        return remote(
            (key, value)[kv].at[pl.ds(block, BLOCK)],
            halo.at[side * 2 + kv],
            hsend.at[side * 2 + kv],
            hrecv.at[side * 2 + kv],
            other,
            head,
        )

    def ring_copy(q, d, t):
        step = 1 if d == 0 else DEPTH - 1
        owner = lax.rem(z + t * (DEPTH - step), DEPTH)
        rows = pl.ds(owner * ITEMS, ITEMS)
        slot = ring_slot(q, d, t)
        return remote(
            held[q].at[rows],
            held[q].at[rows],
            zsend.at[slot],
            zrecv.at[slot],
            lax.rem(z + step, DEPTH) * PLANE + p,
            head,
        )

    def plane_copy(q, i):
        peer = lax.rem(p + i, PLANE)
        return remote(
            out[q].at[pl.ds(peer * c, c)],
            picked[q].at[pl.ds(p * c, c)],
            psend.at[q * PLANE + i],
            precv.at[q * PLANE + i],
            z * PLANE + peer,
            head,
        )

    def offer_copy(i):
        peer = lax.rem(p + i, PLANE)
        return remote(
            offer.at[pl.ds(peer * CHUNKS, CHUNKS)],
            offered.at[pl.ds(p * CHUNKS, CHUNKS)],
            gsend.at[i],
            grecv.at[i],
            z * PLANE + peer,
            head,
        )

    def piece_copy(i):
        other = lax.rem(z + i, DEPTH)
        return remote(
            piece.at[other],
            pieces.at[z],
            gsend.at[PLANE + i],
            grecv.at[PLANE + i],
            other * PLANE + p,
            head,
        )

    def relay_copy(i):
        return remote(
            relay,
            shared.at[z * PLANE + p],
            gsend.at[PLANE + DEPTH + i],
            grecv.at[PLANE + DEPTH + i],
            z * PLANE + lax.rem(p + i, PLANE),
            head,
        )

    def offers(sender, peer):
        return (peer < HEADS_HERE) | (sender == PLANE - 1)

    def offer_start():
        for e in range(PLANE):
            second = (global_block(ids, e) & 1) == 1
            j = e % HEADS_HERE
            for q in range(CHUNKS):
                low, high = [
                    (key, value)[q // PARTS][
                        b * BLOCK + (q % PARTS) * ROWS : b * BLOCK + (q % PARTS + 1) * ROWS,
                        j * HEAD_DIM : (j + 1) * HEAD_DIM,
                    ]
                    for b in range(BLOCKS_HERE)
                ]
                offer[e * CHUNKS + q] = jnp.where(second, high, low)

        @pl.loop(1, PLANE)
        def _(i):
            @pl.when(offers(p, lax.rem(p + i, PLANE)))
            def _():
                offer_copy(i).start()

        mine = pl.ds(p * CHUNKS, CHUNKS)
        offered[mine] = offer[mine]

    def piece_start():
        @pl.loop(1, PLANE)
        def _(i):
            @pl.when(offers(lax.rem(p + PLANE - i, PLANE), p))
            def _():
                offer_copy(i).wait_recv()

        _, column, _ = global_place(ids, p)
        for q in range(CHUNKS):
            found = offered[(PLANE - 1) * CHUNKS + q]
            for source in range(PLANE - 1):
                found = jnp.where(column == source, offered[source * CHUNKS + q], found)
            piece[q] = found

        @pl.loop(1, DEPTH)
        def _(i):
            piece_copy(i).start()

        pieces[z] = piece[z]

    def relay_start():
        @pl.loop(1, DEPTH)
        def _(i):
            piece_copy(i).wait_recv()

        plane, _, _ = global_place(ids, p)
        found = pieces[DEPTH - 1]
        for source in range(DEPTH - 1):
            found = jnp.where(plane == source, pieces[source], found)
        relay[...] = found
        shared[z * PLANE + p] = relay[...]

        @pl.loop(1, PLANE)
        def _(i):
            relay_copy(i).start()

    def relay_wait():
        @pl.loop(1, PLANE)
        def _(i):
            relay_copy(i).wait_recv()

    def fill(q):
        source, part = (key, value)[q // PARTS], q % PARTS
        for b in range(BLOCKS_HERE):
            for j in range(HEADS_HERE):
                held[q][z * ITEMS + b * HEADS_HERE + j] = source[
                    b * BLOCK + part * ROWS : b * BLOCK + (part + 1) * ROWS,
                    j * HEAD_DIM : (j + 1) * HEAD_DIM,
                ]

    def ring_start(q):
        for d in range(2):
            ring_copy(q, d, 0).start()

    def ring_step(q, t):
        for d in range(2):
            if t < ring_hops(q, d):
                ring_copy(q, d, t).wait_recv()
                if t + 1 < ring_hops(q, d):
                    ring_copy(q, d, t + 1).start()

    def spread(q):
        @pl.loop(1, PLANE)
        def _(i):
            peer = lax.rem(p + i, PLANE)
            for s in range(c):
                out[q][peer * c + s] = held[q][slots[peer, 0, s]]
            plane_copy(q, i).start()

        for s in range(c):
            picked[q][p * c + s] = held[q][slots[p, 0, s]]

    fill(0)

    @pl.loop(1, 2 * DEPTH)
    def _(i):
        other = lax.rem(place + i, 2 * DEPTH)
        signal(lax.div(other, 2) * PLANE + p, lax.rem(other, 2))

    @pl.loop(1, PLANE)
    def _(i):
        signal(z * PLANE + lax.rem(p + i, PLANE), head)

    for step in (1, PLANE * DEPTH - 1):
        signal(lax.rem(seq + step, PLANE * DEPTH), head)
    pl.semaphore_wait(pltpu.get_barrier_semaphore(), 2 * DEPTH - 1 + PLANE - 1 + 2)

    ring_start(0)
    fill(1)
    ring_start(1)
    write_tables(c, rand_peer, rand_local, table, where, plan)

    @pl.loop(1, PLANE)
    def _(i):
        table_copy(i).start()

    got[p] = table[p]
    offer_start()
    for q in range(2, CHUNKS):
        fill(q)
    for side in range(2):
        for kv in range(2):
            halo_copy(side, kv).start()

    for step in range(CHUNKS + 4):
        for t in range(3, -1, -1):
            if 0 <= step - t <= CHUNKS:
                ring_step(step - t, t)
        if step + 2 == CHUNKS:
            relay_wait()
        if step + 2 <= CHUNKS:
            ring_start(step + 2)
        if step == 1:
            piece_start()
        if step == 3:
            relay_start()
        if step == 2:

            @pl.loop(1, PLANE)
            def _(i):
                table_copy(i).wait()

            to_scalars = pltpu.make_async_copy(got, slots, local)
            to_scalars.start()
            to_scalars.wait()
        if 0 <= step - 3 < CHUNKS:
            spread(step - 3)
        if step == 4:
            most[place] = jnp.max(got[...], axis=0)

            @pl.loop(1, 2 * DEPTH)
            def _(i):
                most_copy(i).start()

    @pl.loop(1, 2 * DEPTH)
    def _(i):
        most_copy(i).wait()

    peak[...] = jnp.max(most[...], axis=0)
    @pl.loop(1, PLANE)
    def _(i):
        @pl.when(offers(p, lax.rem(p + i, PLANE)))
        def _():
            offer_copy(i).wait_send()

        relay_copy(i).wait_send()

    @pl.loop(1, DEPTH)
    def _(i):
        piece_copy(i).wait_send()

    for q in range(CHUNKS + 1):
        if q < CHUNKS:

            @pl.loop(1, PLANE)
            def _(i):
                plane_copy(q, i).wait()

        for d in range(2):
            for t in range(ring_hops(q, d)):
                ring_copy(q, d, t).wait_send()
    for side in range(2):
        for kv in range(2):
            halo_copy(side, kv).wait()


def fetch(c, ids, rand_peer, rand_local, key, value, collective_id):
    smem = pl.BlockSpec(memory_space=pltpu.SMEM)
    vmem = pl.BlockSpec(memory_space=pltpu.VMEM)
    part = jax.ShapeDtypeStruct((PLANE * c, ROWS, HEAD_DIM), BF16)
    rows = jax.ShapeDtypeStruct((PLANE, 8, 128), jnp.int32)
    dma = pltpu.SemaphoreType.DMA
    return pl.pallas_call(
        functools.partial(fetch_kernel, c),
        out_shape=(
            rows,
            jax.ShapeDtypeStruct((8, 128), jnp.int32),
            jax.ShapeDtypeStruct((PICKS, 128), jnp.int32),
            jax.ShapeDtypeStruct((PLANE, 128), jnp.int32),
            jax.ShapeDtypeStruct((4, BLOCK, WIDTH), BF16),
            jax.ShapeDtypeStruct((CHUNKS * PLANE, ROWS, HEAD_DIM), BF16),
        )
        + (part,) * CHUNKS,
        in_specs=[smem, vmem, vmem, vmem, vmem],
        out_specs=(vmem,) * (6 + CHUNKS),
        scratch_shapes=[pltpu.VMEM((DEPTH * ITEMS, ROWS, HEAD_DIM), BF16)] * CHUNKS
        + [pltpu.VMEM(part.shape, BF16)] * CHUNKS
        + [
            pltpu.VMEM((ROWS, HEAD_DIM), BF16),
            pltpu.VMEM((PLANE * CHUNKS, ROWS, HEAD_DIM), BF16),
            pltpu.VMEM((PLANE * CHUNKS, ROWS, HEAD_DIM), BF16),
            pltpu.VMEM((DEPTH, ROWS, HEAD_DIM), BF16),
            pltpu.VMEM((DEPTH, ROWS, HEAD_DIM), BF16),
            pltpu.SMEM((PLANE, 8, 128), jnp.int32),
            pltpu.VMEM((PLANE, 8, 128), jnp.int32),
            pltpu.VMEM((2 * DEPTH, 8, 128), jnp.int32),
            dma(()),
            dma((7 * (CHUNKS + 1),)),
            dma((7 * (CHUNKS + 1),)),
            dma((CHUNKS * PLANE,)),
            dma((CHUNKS * PLANE,)),
            dma((2 * PLANE + DEPTH,)),
            dma((2 * PLANE + DEPTH,)),
            dma((4,)),
            dma((4,)),
            dma((PLANE,)),
            dma((PLANE,)),
            dma((2 * DEPTH,)),
            dma((2 * DEPTH,)),
        ],
        compiler_params=pltpu.CompilerParams(
            collective_id=collective_id, has_side_effects=True, vmem_limit_bytes=VMEM_BYTES
        ),
        name=f"fetch_{c}",
    )(ids, rand_peer, rand_local, key, value)


def dot(a, b, contract):
    return lax.dot_general(a, b, ((contract[0:1], contract[1:2]), ((), ())), preferred_element_type=F32)


def back_kernel(c, ids, where, plan, order, first, ends, query, grad, key, value, halo, shared, *rest):
    picked, rest = rest[:CHUNKS], rest[CHUNKS:]
    outs, rest = rest[:4], rest[4:]
    terms, rest = rest[:CHUNKS], rest[CHUNKS:]
    out, rest = rest[:CHUNKS], rest[CHUNKS:]
    arrived, rest = rest[:CHUNKS], rest[CHUNKS:]
    totals, rest = rest[:CHUNKS], rest[CHUNKS:]
    (
        attended, grad_query, own, sides, both, weights,
        zone_in, zone, tile_in, extras, relay, runs, zout, zin, beside, cross,
        zsend, zrecv, psend, precv, gsend, grecv, hsend, hrecv, csend, crecv,
    ) = rest
    seq, z, p, head = position()

    @pl.loop(1, PLANE)
    def _(i):
        signal(z * PLANE + lax.rem(p + i, PLANE), head)

    @pl.loop(1, DEPTH)
    def _(i):
        signal(lax.rem(z + i, DEPTH) * PLANE + p, head)

    for step in (1, PLANE * DEPTH - 1):
        signal(lax.rem(seq + step, PLANE * DEPTH), head)
    signal(seq, 1 - head)

    scale = HEAD_DIM ** (-0.5)
    near = 4 * BLOCK
    rows = lax.broadcasted_iota(jnp.int32, (near, 128), 0)
    lanes = lax.broadcasted_iota(jnp.int32, (near, 128), 1)
    hidden = (
        ((lanes < BLOCK) & (rows >= 3 * BLOCK))
        | ((lanes >= BLOCK) & (rows < BLOCK))
        | ((rows < BLOCK) & (seq == 0))
        | ((rows >= 3 * BLOCK) & (seq == PLANE * DEPTH - 1))
    )
    pick_lanes = lax.broadcasted_iota(jnp.int32, (3 * BLOCK, 128), 1) < BLOCK

    def columns_of(j):
        return pl.ds(pl.multiple_of(j * HEAD_DIM, HEAD_DIM), HEAD_DIM)

    def listed(kv, j):
        cols = columns_of(j)
        close = [halo[kv, :, cols], (key, value)[kv][:, cols], halo[2 + kv, :, cols]]
        for group in range(2):
            for part in range(PARTS):
                close.append(shared[(kv * PARTS + part) * PLANE + group * HEADS_HERE + j])
        far = []
        for b in range(BLOCKS_HERE):
            pieces = []
            for t in range(3):
                at = where[t * ITEMS + b * HEADS_HERE + j, 0]
                for part in range(PARTS):
                    pieces.append(picked[kv * PARTS + part][at])
            far.append(jnp.concatenate(pieces, axis=0))
        return jnp.concatenate(close, axis=0), far

    def products(close, far, other):
        a = dot(close, other, (1, 1))
        b = jnp.where(pick_lanes, dot(far[0], other, (1, 1)), dot(far[1], other, (1, 1)))
        return a, b

    def gather(near_w, far_w, close, far):
        total = dot(near_w, close, (0, 0))
        top_rows = dot(far_w, far[0], (0, 0))
        low_rows = dot(far_w, far[1], (0, 0))
        return total + jnp.concatenate([top_rows[:BLOCK], low_rows[BLOCK:]], axis=0)

    def scatter(kv, j, weight_near, weight_far, rows_here):
        near_terms = dot(weight_near, rows_here, (1, 0))
        zero = jnp.zeros_like(weight_far)
        far_terms = (
            dot(jnp.where(pick_lanes, weight_far, zero), rows_here, (1, 0)).astype(BF16),
            dot(jnp.where(pick_lanes, zero, weight_far), rows_here, (1, 0)).astype(BF16),
        )
        for part in range(PARTS):
            chunk = kv * PARTS + part

            def piece(block):
                start = block * BLOCK + part * ROWS
                return near_terms[start : start + ROWS]

            sides[chunk * HEADS_HERE + j] = piece(0).astype(BF16)
            sides[(CHUNKS + chunk) * HEADS_HERE + j] = piece(3).astype(BF16)
            for b in range(BLOCKS_HERE):
                own[chunk * ITEMS + b * HEADS_HERE + j] = piece(1 + b)
                for t in range(3):
                    start = t * BLOCK + part * ROWS
                    terms[chunk][t * ITEMS + b * HEADS_HERE + j] = far_terms[b][start : start + ROWS]
            for group in range(2):
                both[((kv * 2 + group) * HEADS_HERE + j) * PARTS + part] = piece(4 + group).astype(BF16)

    def weigh(j):
        cols = columns_of(j)
        keys, far_keys = listed(0, j)
        s_near, s_far = products(keys, far_keys, query[:, cols])
        s_near = s_near * scale
        s_far = s_far * scale
        s_near = jnp.concatenate(
            [jnp.where(hidden, -1e30, s_near[:near]), s_near[near:]], axis=0
        )
        top = jnp.maximum(
            jnp.max(s_near, axis=0, keepdims=True), jnp.max(s_far, axis=0, keepdims=True)
        )
        w_near = jnp.exp(s_near - top)
        w_far = jnp.exp(s_far - top)
        total = jnp.sum(w_near, axis=0, keepdims=True) + jnp.sum(w_far, axis=0, keepdims=True)
        inverse = 1.0 / total
        w_near = w_near * inverse
        w_far = w_far * inverse
        weights[j, : 6 * BLOCK] = w_near
        weights[j, 6 * BLOCK :] = w_far
        scatter(1, j, w_near.astype(BF16), w_far.astype(BF16), grad[:, cols])

    def backward(j):
        cols = columns_of(j)
        q, g = query[:, cols], grad[:, cols]
        keys, far_keys = listed(0, j)
        values, far_values = listed(1, j)
        w_near, w_far = weights[j, : 6 * BLOCK], weights[j, 6 * BLOCK :]
        gw_near, gw_far = products(values, far_values, g)
        centre = jnp.sum(w_near * gw_near, axis=0, keepdims=True) + jnp.sum(
            w_far * gw_far, axis=0, keepdims=True
        )
        d_near = (w_near * (gw_near - centre) * scale).astype(BF16)
        d_far = (w_far * (gw_far - centre) * scale).astype(BF16)
        scatter(0, j, d_near, d_far, q)
        attended[:, cols] = gather(
            w_near.astype(BF16), w_far.astype(BF16), values, far_values
        ).astype(BF16)
        grad_query[:, cols] = gather(d_near, d_far, keys, far_keys).astype(BF16)

    count = PLANE * c
    mine = pl.ds(pl.multiple_of(head * WIDTH, WIDTH), WIDTH)

    def result_copy(k):
        source = (attended, grad_query)[k].at[pl.ds((1 - head) * BLOCK, BLOCK)]
        return remote(source, outs[k].at[:, mine], csend.at[k], crecv.at[k], seq, 1 - head)

    def cross_copy(q):
        return remote(
            cross.at[q],
            outs[2 + q // PARTS].at[pl.ds((q % PARTS) * ROWS, ROWS), mine],
            csend.at[2 + q],
            crecv.at[2 + q],
            seq,
            1 - head,
        )

    def side_copy(kv, side):
        size = PARTS * HEADS_HERE
        other = lax.rem(seq + (PLANE * DEPTH - 1 if side == 0 else 1), PLANE * DEPTH)
        return remote(
            sides.at[pl.ds((side * 2 + kv) * size, size)],
            beside.at[pl.ds(((1 - side) * 2 + kv) * size, size)],
            hsend.at[kv * 2 + side],
            hrecv.at[kv * 2 + side],
            other,
            head,
        )

    def plane_copy(q, i):
        peer = lax.rem(p + i, PLANE)
        return remote(
            out[q].at[pl.ds(peer * c, c)],
            arrived[q].at[pl.ds(p * c, c)],
            psend.at[q * PLANE + i],
            precv.at[q * PLANE + i],
            z * PLANE + peer,
            head,
        )

    def zone_copy(kv, i):
        other = lax.rem(z + i, DEPTH)
        rows = pl.ds((kv * PLANE + other * 2) * PARTS, 2 * PARTS)
        return remote(
            both.at[rows],
            zone_in.at[pl.ds((kv * DEPTH + z) * 2 * PARTS, 2 * PARTS)],
            gsend.at[kv * DEPTH + i],
            grecv.at[kv * DEPTH + i],
            other * PLANE + p,
            head,
        )

    def tile_copy(kv, i):
        peer = lax.rem(p + i, PLANE)
        return remote(
            zone.at[kv * 2 * PARTS + lax.rem(peer, 2 * PARTS)],
            tile_in.at[p],
            gsend.at[2 * DEPTH + i],
            grecv.at[2 * DEPTH + i],
            z * PLANE + peer,
            head,
        )

    def total_copy(i):
        peer = lax.rem(p + i, PLANE)
        return remote(
            relay,
            extras.at[z * PLANE + p],
            gsend.at[2 * DEPTH + PLANE + i],
            grecv.at[2 * DEPTH + PLANE + i],
            z * PLANE + peer,
            head,
        )

    def adds(kv, q):
        return lax.div(q, 2 * PARTS) == 1 - kv

    def zone_start(kv):
        @pl.loop(1, DEPTH)
        def _(i):
            zone_copy(kv, i).start()

    def zone_add(kv):
        @pl.loop(1, DEPTH)
        def _(i):
            zone_copy(kv, i).wait_recv()

        size = 2 * PARTS
        total = both[pl.ds((kv * PLANE + z * 2) * PARTS, size)].astype(F32)
        for i in range(1, DEPTH):
            other = lax.rem(z + i, DEPTH)
            total = total + zone_in[pl.ds((kv * DEPTH + other) * size, size)].astype(F32)
        zone[kv * size : (kv + 1) * size] = total.astype(BF16)

        @pl.loop(1, PLANE)
        def _(i):
            @pl.when(adds(kv, lax.rem(p + i, PLANE)))
            def _():
                tile_copy(kv, i).start()

    def tile_add(kv):
        @pl.when(adds(kv, p))
        def _():
            @pl.loop(1, PLANE)
            def _(i):
                tile_copy(kv, i).wait_recv()

            tile_in[p] = zone[kv * 2 * PARTS + lax.rem(p, 2 * PARTS)]
            total = tile_in[0].astype(F32)
            for i in range(1, PLANE):
                total = total + tile_in[i].astype(F32)
            relay[...] = total.astype(BF16)
            extras[z * PLANE + p] = relay[...]

            @pl.loop(1, PLANE)
            def _(i):
                total_copy(i).start()

    def extra_copy(kv, d, t):
        step = 1 if d == 0 else DEPTH - 1
        owner = lax.rem(z + t * (DEPTH - step), DEPTH)
        rows = pl.ds(owner * PLANE + (1 - kv) * 2 * PARTS, 2 * PARTS)
        slot = ring_slot(CHUNKS + kv, d, t)
        return remote(
            extras.at[rows],
            extras.at[rows],
            zsend.at[slot],
            zrecv.at[slot],
            lax.rem(z + step, DEPTH) * PLANE + p,
            head,
        )

    def extra_step(kv, t):
        for d in range(2):
            hops = ring_hops(CHUNKS + kv, d)
            if 0 < t <= hops:
                extra_copy(kv, d, t - 1).wait_recv()
            if t < hops:
                extra_copy(kv, d, t).start()

    def total_wait(kv):
        @pl.loop(1, PLANE)
        def _(i):
            @pl.when(adds(kv, lax.rem(p + PLANE - i, PLANE)))
            def _():
                total_copy(i).wait_recv()

    def ring_copy(q, d, t):
        step = 1 if d == 0 else DEPTH - 1
        slot = ring_slot(q, d, t)
        return remote(
            zout.at[slot],
            zin.at[slot],
            zsend.at[slot],
            zrecv.at[slot],
            lax.rem(z + step, DEPTH) * PLANE + p,
            head,
        )

    def spread(q):
        @pl.loop(1, PLANE)
        def _(i):
            peer = lax.rem(p + i, PLANE)
            for s in range(c):
                out[q][peer * c + s] = terms[q][plan[peer, 3 * LANES + s]]
            plane_copy(q, i).start()

        for s in range(c):
            arrived[q][p * c + s] = terms[q][plan[p, 3 * LANES + s]]

    def collect(q):
        @pl.loop(1, PLANE)
        def _(i):
            plane_copy(q, i).wait_recv()

        def add(r, total):
            term = arrived[q][order[r]].astype(F32)
            total = jnp.where(first[r] == 1, term, total + term)
            runs[r] = total
            return total

        lax.fori_loop(0, count, add, jnp.zeros((ROWS, HEAD_DIM), F32), unroll=8)

        @pl.loop(0, DEPTH * ITEMS, unroll=8)
        def _(i):
            totals[q][i] = runs[ends[i]]

    def ring_step(q, t):
        for d in range(2):
            hops = ring_hops(q, d)
            if t < hops:
                away = hops - t
                target = lax.rem(z + (away if d == 0 else DEPTH - away), DEPTH)
                partial = totals[q][pl.ds(target * ITEMS, ITEMS)]
                if t > 0:
                    ring_copy(q, d, t - 1).wait_recv()
                    partial = partial + zin[ring_slot(q, d, t - 1)].astype(F32)
                zout[ring_slot(q, d, t)] = partial.astype(BF16)
                ring_copy(q, d, t).start()

    def finish(q):
        for d in range(2):
            ring_copy(q, d, ring_hops(q, d) - 1).wait_recv()
        kv, part = q // PARTS, q % PARTS
        for j in range(HEADS_HERE):
            for stays in range(2):
                b = head if stays else 1 - head
                item = b * HEADS_HERE + j
                total = totals[q][z * ITEMS + item] + own[q * ITEMS + item]
                total = total + beside[(b * CHUNKS + q) * HEADS_HERE + j].astype(F32)
                for d in range(2):
                    total = total + zin[ring_slot(q, d, ring_hops(q, d) - 1), item].astype(F32)
                for group in range(2):
                    e = group * HEADS_HERE + j
                    tile = (e // 2) * PLANE + (1 - kv) * 2 * PARTS + (e % 2) * PARTS + part
                    mine_too = global_block(ids, e) == seq * BLOCKS_HERE + b
                    total = total + jnp.where(mine_too, extras[tile].astype(F32), 0.0)
                total = total.astype(BF16)
                if stays:
                    cols = pl.ds(pl.multiple_of(head * WIDTH + j * HEAD_DIM, HEAD_DIM), HEAD_DIM)
                    outs[2 + kv][part * ROWS : (part + 1) * ROWS, cols] = total
                else:
                    cross[q, :, j * HEAD_DIM : (j + 1) * HEAD_DIM] = total
        cross_copy(q).start()

    @pl.loop(0, HEADS_HERE)
    def _(j):
        weigh(j)

    runs[count] = jnp.zeros((ROWS, HEAD_DIM), F32)
    pl.semaphore_wait(pltpu.get_barrier_semaphore(), PLANE + DEPTH + 1)
    turn = list(range(PARTS, CHUNKS)) + list(range(PARTS))
    zone_start(1)
    spread(turn[0])

    @pl.loop(0, HEADS_HERE)
    def _(j):
        backward(j)

    zone_start(0)
    spread(turn[1])
    zone_add(1)
    spread(turn[2])
    for k in range(2):
        result_copy(k).start()
        outs[k][:, mine] = (attended, grad_query)[k][pl.ds(pl.multiple_of(head * BLOCK, BLOCK), BLOCK)]
    for step in range(CHUNKS + 5):
        if 0 < step and step + 2 < CHUNKS:
            spread(turn[step + 2])
        if step == CHUNKS - 3:
            for kv in (1, 0):
                for side in range(2):
                    side_copy(kv, side).start()
        if step == 1:
            tile_add(1)
            zone_add(0)
        if step == 3:
            tile_add(0)
            total_wait(1)
        if step == 5:
            total_wait(0)
        for kv in range(2):
            if 0 <= step - (5 - 2 * kv) <= 4:
                extra_step(kv, step - (5 - 2 * kv))
        for t in range(3, 0, -1):
            if 0 <= step - t < CHUNKS:
                ring_step(turn[step - t], t)
        if step < CHUNKS:
            collect(turn[step])
            ring_step(turn[step], 0)
        for n, q in enumerate(turn):
            if step == (9, 9, 9, 10, 10, 10, 11, 11)[n]:
                if n % PARTS == 0:
                    for side in range(2):
                        side_copy(q // PARTS, side).wait()
                finish(q)
    for kv in range(2):

        @pl.loop(1, DEPTH)
        def _(i):
            zone_copy(kv, i).wait_send()

        @pl.loop(1, PLANE)
        def _(i):
            @pl.when(adds(kv, lax.rem(p + i, PLANE)))
            def _():
                tile_copy(kv, i).wait_send()

    @pl.loop(1, PLANE)
    def _(i):
        total_copy(i).wait_send()

    for kv in range(2):
        for d in range(2):
            for t in range(ring_hops(CHUNKS + kv, d)):
                extra_copy(kv, d, t).wait_send()
    for q in range(CHUNKS):

        @pl.loop(1, PLANE)
        def _(i):
            plane_copy(q, i).wait_send()

        for d in range(2):
            for t in range(ring_hops(q, d)):
                ring_copy(q, d, t).wait_send()
        cross_copy(q).wait()
    for k in range(2):
        result_copy(k).wait()


def back(c, scalars, arrays, picked, collective_id):
    smem = pl.BlockSpec(memory_space=pltpu.SMEM)
    vmem = pl.BlockSpec(memory_space=pltpu.VMEM)
    dma = pltpu.SemaphoreType.DMA
    vm = pltpu.VMEM
    tile = (ROWS, HEAD_DIM)
    part = (PLANE * c,) + tile
    return pl.pallas_call(
        functools.partial(back_kernel, c),
        out_shape=(jax.ShapeDtypeStruct((BLOCK, 2 * WIDTH), BF16),) * 4,
        in_specs=[smem] * len(scalars) + [vmem] * (len(arrays) + CHUNKS),
        out_specs=(vmem,) * 4,
        scratch_shapes=[vm((PICKS,) + tile, BF16)] * CHUNKS
        + [vm(part, BF16)] * (2 * CHUNKS)
        + [vm((DEPTH * ITEMS,) + tile, F32)] * CHUNKS
        + [
            vm((BLOCKS_HERE * BLOCK, WIDTH), BF16),
            vm((BLOCKS_HERE * BLOCK, WIDTH), BF16),
            vm((CHUNKS * ITEMS,) + tile, F32),
            vm((2 * CHUNKS * HEADS_HERE,) + tile, BF16),
            vm((CHUNKS * PLANE,) + tile, BF16),
            vm((HEADS_HERE, 9 * BLOCK, 128), F32),
            vm((2 * DEPTH * 2 * PARTS,) + tile, BF16),
            vm((2 * 2 * PARTS,) + tile, BF16),
            vm((PLANE,) + tile, BF16),
            vm((DEPTH * PLANE,) + tile, BF16),
            vm(tile, BF16),
            vm((PLANE * c + 1,) + tile, F32),
            vm((7 * CHUNKS, ITEMS) + tile, BF16),
            vm((7 * CHUNKS, ITEMS) + tile, BF16),
            vm((2 * CHUNKS * HEADS_HERE,) + tile, BF16),
            vm((CHUNKS, ROWS, WIDTH), BF16),
            dma((7 * (CHUNKS + 2),)),
            dma((7 * (CHUNKS + 2),)),
            dma((CHUNKS * PLANE,)),
            dma((CHUNKS * PLANE,)),
            dma((2 * DEPTH + 2 * PLANE,)),
            dma((2 * DEPTH + 2 * PLANE,)),
            dma((4,)),
            dma((4,)),
            dma((2 + CHUNKS,)),
            dma((2 + CHUNKS,)),
        ],
        compiler_params=pltpu.CompilerParams(
            collective_id=collective_id, has_side_effects=True, vmem_limit_bytes=VMEM_BYTES
        ),
        name=f"back_{c}",
    )(*scalars, *arrays, *picked)


def on_device(
    query_vectors, key_vectors, value_vectors, cotangent, rand_peer, rand_local, global_ids
):
    none = DEPTH * ITEMS
    all_items = jnp.arange(none, dtype=jnp.int32)

    def go(c, collective_id, peers, spots, key, value):
        return fetch(c, global_ids, peers, spots, key, value, collective_id)

    def finish(c, collective_id, query, key, value, grad, fetched):
        got, _, where, plan, halo, shared, *picked = fetched
        count = PLANE * c
        keys = got[:, 0, 2 * LANES : 2 * LANES + c].reshape(count)
        at = jnp.arange(count, dtype=jnp.int32)
        same = keys[None, :] == keys[:, None]
        ahead = at[None, :] < at[:, None]
        before = (keys[None, :] < keys[:, None]) | (same & ahead)
        sorted_at = jnp.sum(before.astype(jnp.int32), axis=1)
        chosen = sorted_at[None, :] == at[:, None]
        order = jnp.sum(jnp.where(chosen, at[None, :], 0), axis=1)
        opens = ~jnp.any(same & ahead, axis=1)
        first = jnp.sum(jnp.where(chosen & opens[None, :], 1, 0), axis=1)
        upto = jnp.sum((keys[None, :] <= all_items[:, None]).astype(jnp.int32), axis=1)
        found = jnp.any(keys[None, :] == all_items[:, None], axis=1)
        ends = jnp.where(found, upto - 1, count)
        return back(
            c,
            (global_ids, where, plan, order, first, ends),
            (query, grad, key, value, halo, shared),
            picked,
            collective_id,
        )

    def usual(query, key, value, grad, peers, spots, *fetched):
        return finish(USUAL, 1, query, key, value, grad, fetched)

    def crowded(query, key, value, grad, peers, spots, *fetched):
        return finish(FULL, 3, query, key, value, grad, go(FULL, 2, peers, spots, key, value))

    fetched = go(USUAL, 0, rand_peer, rand_local, key_vectors, value_vectors)
    return lax.cond(
        fetched[1][0, LANES] > USUAL, crowded, usual,
        query_vectors, key_vectors, value_vectors, cotangent, rand_peer, rand_local, *fetched,
    )


def solution(mesh):
    placed = (
        P("seq", "head"),
        P("seq", "head"),
        P("seq", "head"),
        P("seq", "head"),
        P("head", "seq", None, None),
        P("head", "seq", None, None),
        P(),
    )
    return jax.shard_map(
        on_device,
        mesh=mesh,
        in_specs=placed,
        out_specs=(P(("seq", "head"), None),) * 4,
        check_vma=False,
    )
```
